32 devices in a mesh: leaf: 32 (over z, y, x, core).
Axes of the slice: x: 2, y: 2, z: 4, core: 2. Of those that a mesh axis runs over, the one named last changes fastest.
Arguments:
- points: bfloat16 [64, 131072], P(None, 'leaf'), may hold values from -5 to 5
- charges: bfloat16 [32, 131072], P(None, 'leaf'), may hold values from -1.5 to 1.5
- leaf_order: int32 [32, 4096], P('leaf'), may hold values from 0 to 4095, each once within a row
- near_list: int32 [512, 16], P('leaf'), may hold values from -1 to 511, as said below
- far_list: int32 [256, 8], P('leaf'), may hold values from -1 to 7
- local_skel: int32 [480, 256], P('leaf'), may hold values from 0 to 511, as said below
- upper_skel: int32 [30, 256], replicated, may hold values from 0 to 511, as said below
Outputs:
- potentials: float32 [32, 131072], P(None, 'leaf')
- root_field: float32 [32, 32, 256], P('leaf')
The draws below stay inside these ranges and needn't reach their ends.
Inputs may be any that keep to these rules, and one draw needn't show every extreme that they name: `leaf_order`: each row is a permutation of the positions of one device's points. `near_list`: slot 0 of leaf g's row is g itself; every other entry is -1 or a leaf h different from g with |h - g| <= 16, and the leaves of one row are distinct. `far_list`: an entry other than -1 names a level-one node of the same device subtree, counted from that subtree's first level-one node; entries of a row may repeat. `local_skel`: the entries of a row are distinct. `upper_skel`: the entries of a row are distinct.
All inputs are finite; a program needn't handle non-finite values.
Results may differ from the reference program's by a relative error of at most 0.0014.
Values may be sent and summed in bfloat16 or wider, within the bound.
No kernel may reach another device: no remote copies, remote signals or barrier semaphores. Data moves between devices by JAX's collectives and lax.ppermute only.
A program may use at most 64 MiB of HBM per device.

```python
import math
import jax
import jax.numpy as jnp
from jax import lax

FEAT = 64
LEAF_PTS = 256
SKEL = 256
RHS = 32
NEAR = 16
FAR = 8
LEAF_DEV = 16
LOCAL_LEV = 4
UPPER = 5
PTS_DEV = 4096
LEAVES = 512
POINTS = 131072
N_LEAF = 32


def distinct_rows(key, row_count, pool_size, count_taken):
    scores = jax.random.randint(key, (row_count, pool_size), 0, 1 << 20) * pool_size
    scores = scores + jnp.arange(pool_size, dtype=jnp.int32)[None, :]
    return jnp.argsort(scores, axis=1)[:, :count_taken].astype(jnp.int32)


def draw_near_list(key, part):
    leaf_total = N_LEAF * LEAF_DEV
    picks = distinct_rows(jax.random.fold_in(key, 7), leaf_total, 2 * LEAF_DEV, NEAR - 1)
    offsets = jnp.where(picks < LEAF_DEV, picks - LEAF_DEV, picks - LEAF_DEV + 1)
    self_ids = jnp.arange(leaf_total, dtype=jnp.int32)[:, None]
    others = self_ids + offsets
    dropped = jax.random.randint(jax.random.fold_in(key, 8), (leaf_total, NEAR - 1), 0, 8) == 0
    others = jnp.where((others < 0) | (others >= leaf_total) | dropped, -1, others)
    others = others.at[0, NEAR - 2].set(-1)
    return jnp.concatenate([self_ids, others], axis=1).astype(jnp.int32)


def draw_local_skel(key, part):
    return distinct_rows(jax.random.fold_in(key, 11), N_LEAF * (LEAF_DEV - 1), 2 * SKEL, SKEL)


def draw_upper_skel(key, part):
    return distinct_rows(jax.random.fold_in(key, 13), N_LEAF - 2, 2 * SKEL, SKEL)


def touch_ends(drawn, rng, low, largest):
    place = [jax.random.randint(jax.random.fold_in(rng, axis), (), 0, length) for axis, length in enumerate(drawn.shape)]
    main_axis = drawn.shape.index(max(drawn.shape))
    neighbour = place[:main_axis] + [(place[main_axis] + 1) % drawn.shape[main_axis]] + place[main_axis + 1:]
    return drawn.at[tuple(place)].set(low).at[tuple(neighbour)].set(largest)


def shard_levels(own_key, shape, pieces, smallest, top_value):
    def one(axis_at, shards_of):
        draws = jax.random.uniform(jax.random.fold_in(jax.random.fold_in(own_key, 6), axis_at), (shards_of,), jnp.float32, smallest / len(pieces), top_value / len(pieces))
        return jnp.repeat(jnp.exp(draws), shape[axis_at] // shards_of).reshape((-1,) + (1,) * (len(shape) - axis_at - 1))

    factor_of = one(*pieces[0])
    for cut in pieces[1:]:
        factor_of = factor_of * one(*cut)
    return factor_of


def normal_values(stream_key, dims, scale, limit, split=(), held_as=jnp.bfloat16):
    values = jax.random.normal(stream_key, dims, jnp.float32) * scale
    if len(split) > 0:
        values = shard_levels(stream_key, dims, split, -0.22, 0.18) * values
    return jnp.clip(values, min=-limit, max=limit).astype(held_as)


def setup_inputs(seed: int = 0) -> dict:
    splits = jax.random.split(jax.random.key(seed), 8)
    return {
        "points": normal_values(splits[0], (FEAT, POINTS), 1.0, 5.0, ((1, 32),)),
        "charges": normal_values(splits[1], (RHS, POINTS), 0.25, 1.5, ((1, 32),)),
        "leaf_order": jax.vmap(lambda own: jax.random.permutation(own, PTS_DEV))(jax.random.split(splits[2], N_LEAF)).reshape((N_LEAF, PTS_DEV)).astype(jnp.int32),
        "near_list": draw_near_list(jax.random.fold_in(splits[7], 71), 0),
        "far_list": touch_ends(jax.random.randint(splits[4], (LEAVES // 2, FAR), -1, LEAF_DEV // 2), jax.random.fold_in(splits[4], 1), -1, (LEAF_DEV // 2) - 1).astype(jnp.int32),
        "local_skel": draw_local_skel(jax.random.fold_in(splits[7], 71), 0),
        "upper_skel": draw_upper_skel(jax.random.fold_in(splits[7], 71), 0),
    }


pair_gain = math.sqrt(2.0)

def matern(source, target, kern_scale):
    inner_prod = lax.dot_general(source, target, (((0,), (0,)), ((), ())), preferred_element_type=jnp.float32)
    source_sq = lax.optimization_barrier(jnp.sum(jnp.square(source.astype(jnp.float32)), axis=0))
    target_sq = lax.optimization_barrier(jnp.sum(jnp.square(target.astype(jnp.float32)), axis=0))
    spread = jnp.maximum(source_sq[:, None] + target_sq[None, :] - 2.0 * inner_prod, 0.0)
    radius = jnp.sqrt(spread) * kern_scale
    return ((1.0 + radius) * jnp.exp(-radius)).astype(jnp.bfloat16)

def transfer(source, target, weights, kern_scale):
    return jnp.dot(weights, matern(source, target, kern_scale), preferred_element_type=jnp.float32)

def averaged(source, target, weights, kern_scale):
    kernel = matern(source, target, kern_scale)
    column_total = lax.optimization_barrier(jnp.sum(kernel.astype(jnp.float32), axis=0))
    return jnp.dot(weights, kernel, preferred_element_type=jnp.float32) / column_total[None, :]

def join_halves(stacked):
    node_count, row_count, col_count = stacked.shape
    paired = stacked.reshape(node_count // 2, 2, row_count, col_count).transpose(0, 2, 1, 3)
    return paired.reshape(node_count // 2, row_count, 2 * col_count)

def split_halves(joined):
    node_count, row_count, col_count = joined.shape
    halves = joined.reshape(node_count, row_count, 2, col_count // 2).transpose(0, 2, 1, 3)
    return halves.reshape(2 * node_count, row_count, col_count // 2)

def reference(points, charges, leaf_order, near_list, far_list, local_skel, upper_skel):
    kern_scale = 2.0 * math.sqrt(3.0 / FEAT)
    leaf_total = N_LEAF * LEAF_DEV
    top_height = LOCAL_LEV + UPPER
    tree_order = (leaf_order + (jnp.arange(N_LEAF, dtype=jnp.int32) * PTS_DEV)[:, None]).reshape(-1)
    leaf_points = jnp.take(points, tree_order, axis=1).reshape(FEAT, leaf_total, LEAF_PTS).transpose(1, 0, 2)
    leaf_charges = jnp.take(charges, tree_order, axis=1).reshape(RHS, leaf_total, LEAF_PTS).transpose(1, 0, 2)

    def near_one(bundle):
        target, slot_ids = bundle

        def add_slot(running, slot_id):
            safe_id = jnp.maximum(slot_id, 0)
            contribution = transfer(leaf_points[safe_id], target, leaf_charges[safe_id], kern_scale)
            return (running + contribution * (slot_id >= 0).astype(jnp.float32), None)
        row_total, _ = lax.scan(add_slot, jnp.zeros((RHS, LEAF_PTS), jnp.float32), slot_ids)
        return row_total
    near_field = lax.map(near_one, (leaf_points, near_list))

    def lift_node(bundle):
        return (pair_gain * averaged(bundle[0], bundle[1], bundle[2], kern_scale)).astype(jnp.bfloat16)

    def couple_node(bundle):
        return transfer(bundle[0], bundle[1], bundle[2], kern_scale)

    def push_node(bundle):
        return averaged(bundle[0], bundle[1], bundle[2].astype(jnp.bfloat16), kern_scale)
    node_points = [leaf_points]
    node_weights = [leaf_charges]
    joined_points = [None]
    for height in range(1, top_height):
        pair_points = join_halves(node_points[-1])
        pair_weights = join_halves(node_weights[-1])
        node_count = leaf_total >> height
        node_ids = jnp.arange(node_count, dtype=jnp.int32)
        if height <= LOCAL_LEV:
            per_device = LEAF_DEV >> height
            table_rows = node_ids // per_device * (LEAF_DEV - 1) + (LEAF_DEV - (LEAF_DEV >> height - 1)) + node_ids % per_device
            chosen = local_skel[table_rows]
        else:
            table_rows = N_LEAF - (N_LEAF >> height - LOCAL_LEV - 1) + node_ids
            chosen = upper_skel[table_rows]
        parent_points = jnp.take_along_axis(pair_points, chosen[:, None, :], axis=2)
        parent_weights = lax.map(lift_node, (pair_points, parent_points, pair_weights))
        node_points.append(parent_points)
        node_weights.append(parent_weights)
        joined_points.append(pair_points)
    fields = [None] * top_height
    for height in range(1, top_height):
        here_points = node_points[height]
        here_weights = node_weights[height]
        partner = jnp.arange(here_points.shape[0], dtype=jnp.int32) ^ 1
        coupled = lax.map(couple_node, (here_points[partner], here_points, here_weights[partner]))
        if height == 1:
            per_node = LEAF_DEV // 2
            base_ids = jnp.arange(leaf_total // 2, dtype=jnp.int32) // per_node * per_node

            def far_one(bundle):
                target, entries, base_id = bundle

                def add_entry(running, entry):
                    safe_id = base_id + jnp.maximum(entry, 0)
                    contribution = transfer(here_points[safe_id], target, here_weights[safe_id], kern_scale)
                    return (running + contribution * (entry >= 0).astype(jnp.float32), None)
                row_total, _ = lax.scan(add_entry, jnp.zeros((RHS, SKEL), jnp.float32), entries)
                return row_total
            coupled = coupled + lax.map(far_one, (here_points, far_list, base_ids))
        fields[height] = coupled
    leaf_field = None
    root_field = None
    for height in range(top_height - 1, 0, -1):
        if height == LOCAL_LEV:
            root_field = fields[height]
        pushed = lax.map(push_node, (node_points[height], joined_points[height], fields[height]))
        spread = split_halves(pushed)
        if height > 1:
            fields[height - 1] = fields[height - 1] + spread
        else:
            leaf_field = spread
    tree_rows = (leaf_field + near_field).transpose(1, 0, 2).reshape(RHS, POINTS)
    potentials = jnp.zeros((RHS, POINTS), jnp.float32).at[:, tree_order].set(tree_rows)
    return (potentials, root_field)
```

```python
import functools
import math

import jax
import jax.numpy as jnp
from jax import lax
from jax.experimental import pallas as pl
from jax.experimental.pallas import tpu as pltpu
from jax.sharding import PartitionSpec as P

PAIR_GAIN = math.sqrt(2.0)
LOG2E = math.log2(math.e)
BF = jnp.bfloat16
F32 = jnp.float32
NT = (((1,), (1,)), ((), ()))
AUX = 8
DEPTH = 128
BATCH = 8
VMEM = pl.BlockSpec(memory_space=pltpu.VMEM)
SMEM = pl.BlockSpec(memory_space=pltpu.SMEM)


def nt_dot(a, b):
    return lax.dot_general(a, b, NT, preferred_element_type=F32)


def nn_dot(a, b):
    return jnp.dot(a, b, preferred_element_type=F32)


def call(body, out_shape, in_specs, scratch, flops, limit_mb=24):
    return pl.pallas_call(
        body,
        out_shape=out_shape,
        in_specs=in_specs,
        out_specs=jax.tree.map(lambda _: VMEM, out_shape),
        scratch_shapes=scratch,
        compiler_params=pltpu.CompilerParams(vmem_limit_bytes=limit_mb * 2**20),
        cost_estimate=pl.CostEstimate(flops=flops, bytes_accessed=2**20, transcendentals=0),
    )


def kernel_tile(sq_dist, kern_scale):
    floor = jnp.maximum(sq_dist, 1e-30)
    root = floor * lax.rsqrt(floor)
    decay = jnp.exp2(root * (-kern_scale * LOG2E))
    return ((1.0 + root * kern_scale) * decay).astype(BF)


def aux_rows(x):
    width = x.shape[1]
    norm = jnp.sum(x * x, axis=0, keepdims=True)
    high = norm.astype(BF).astype(F32)
    rest = norm - high
    mid = rest.astype(BF).astype(F32)
    low = rest - mid
    row = lax.broadcasted_iota(jnp.int32, (AUX, width), 0)
    norms = jnp.where(row == 0, high, jnp.where(row == 1, mid, jnp.where(row == 2, low, 0.0)))
    ones = jnp.where(row < 3, 1.0, 0.0)
    return norms, ones


def source_form(x, norms, ones):
    pad = jnp.zeros((DEPTH - x.shape[0] - 2 * AUX, x.shape[1]), F32)
    return jnp.concatenate([x, norms, ones, pad], axis=0).astype(BF)


def target_form(x, norms, ones):
    pad = jnp.zeros((DEPTH - x.shape[0] - 2 * AUX, x.shape[1]), F32)
    return jnp.concatenate([-2.0 * x, ones, norms, pad], axis=0).T.astype(BF)


def split_form(selected, features):
    return (
        selected[:features],
        selected[features : features + AUX],
        selected[features + AUX : features + 2 * AUX],
    )


def one_hot(chosen, height):
    width = chosen.shape[1]
    row = lax.broadcasted_iota(jnp.int32, (height, width), 0)
    return jnp.where(row == chosen, 1.0, 0.0).astype(BF)


def gather_kernel(points, charges, order, stacked, grid, hots):
    features, total = points.shape
    rows = stacked.shape[0]
    width = hots.shape[1]
    blocks = total // width
    for b in range(blocks):
        cols = pl.ds(b * width, width)
        grid[b, :features] = points[:, cols]
        grid[b, features:] = charges[:, cols]
    for b in range(blocks):
        hots[b] = one_hot(order[:, pl.ds(b * width, width)] & (width - 1), width)

    def block(j, carry):
        start = pl.multiple_of(j * width, width)
        home = order[:, pl.ds(start, width)] // width
        spread = nn_dot(grid[...].reshape(blocks * rows, width), hots[j])
        total_rows = jnp.zeros((rows, width), F32)
        for b in range(blocks):
            mask = jnp.where(home == b, 1.0, 0.0)
            total_rows = total_rows + spread[b * rows : (b + 1) * rows] * mask
        stacked[:, pl.ds(start, width)] = total_rows.astype(BF)
        return carry

    lax.fori_loop(0, blocks, block, 0)


def lift(sources, weights, target, kern_scale):
    kernel = kernel_tile(nn_dot(target, sources), kern_scale)
    sums = nt_dot(weights, kernel)
    rhs = weights.shape[0] - 16
    lifted = PAIR_GAIN * (sums[:rhs] / sums[rhs : rhs + 1])
    return kernel, lifted


def with_ones(weights):
    return jnp.concatenate([weights, jnp.ones((16, weights.shape[1]), weights.dtype)], axis=0)


def tree_kernel(
    kern_scale, features, stacked, skel,
    leaf_src, leaf_tgt, leaf_wts, src1, tgt1, wts1, src_up, tgt_up, wts_up, kernels, payload,
    joined, joined_w,
):
    leaves = leaf_src.shape[0]
    width = leaf_src.shape[2]
    for leaf in range(leaves):
        cols = pl.ds(leaf * width, width)
        x = stacked[:features, cols].astype(F32)
        norms, ones = aux_rows(x)
        leaf_src[leaf] = source_form(x, norms, ones)
        leaf_tgt[leaf] = target_form(x, norms, ones)
        leaf_wts[leaf] = stacked[features:, cols]
    depth = leaves.bit_length() - 1
    live = features + 2 * AUX
    row = 0
    for height in range(1, depth + 1):
        for node in range(leaves >> height):
            if height == 1:
                src, wts, first = leaf_src, leaf_wts, 2 * node
            elif height == 2:
                src, wts, first = src1, wts1, 2 * node
            else:
                below = (leaves // 2) - (leaves >> (height - 2))
                src, wts, first = src_up, wts_up, below + 2 * node
            slot = row % 8
            for half in range(2):
                joined[slot, :, half * width : (half + 1) * width] = src[first + half]
                joined_w[slot, :, half * width : (half + 1) * width] = with_ones(wts[first + half])
            hot = one_hot(skel[row : row + 1, :], 2 * width)
            x, norms, ones = split_form(nn_dot(joined[slot, :live], hot), features)
            own_src = source_form(x, norms, ones)
            own_tgt = target_form(x, norms, ones)
            kernel, lifted = lift(joined[slot], joined_w[slot], own_tgt, kern_scale)
            kernels[row] = kernel
            own_wts = lifted.astype(BF)
            if height == 1:
                src1[node], tgt1[node], wts1[node] = own_src, own_tgt, own_wts
            else:
                at = row - leaves // 2
                src_up[at], tgt_up[at], wts_up[at] = own_src, own_tgt, own_wts
            if height == depth:
                payload[:live] = own_src[:live]
                payload[live:] = own_wts
            row += 1


def padded(rows):
    return jnp.concatenate(
        [rows, jnp.zeros((DEPTH - rows.shape[0], rows.shape[1]), rows.dtype)], axis=0
    )


def couple_kernel(kern_scale, live, sibling, own_tgt, field):
    kernel = kernel_tile(nn_dot(own_tgt[...], padded(sibling[:live])), kern_scale)
    field[...] = nt_dot(sibling[live:], kernel)


def chain_kernel(
    kern_scale, features, place, own, sibling, own_tgt, skel,
    field, next_own, next_tgt, half_kernel, joined, joined_w,
):
    live = features + 2 * AUX
    width = own.shape[1]
    kernel = kernel_tile(nn_dot(own_tgt[...], padded(sibling[:live])), kern_scale)
    field[...] = nt_dot(sibling[live:], kernel)
    joined[:, :width] = padded(own[:live])
    joined[:, width:] = padded(sibling[:live])
    joined_w[:, :width] = with_ones(own[live:])
    joined_w[:, width:] = with_ones(sibling[live:])
    chosen = skel[pl.ds(place[0], 1), :]
    chosen = chosen + place[1] * jnp.where(chosen < width, width, -width)
    hot = one_hot(chosen, 2 * width)
    x, norms, ones = split_form(nn_dot(joined[:live], hot), features)
    target = target_form(x, norms, ones)
    kernel, lifted = lift(joined[...], joined_w[...], target, kern_scale)
    half_kernel[...] = kernel[:, :width]
    next_tgt[...] = target
    next_own[:live] = source_form(x, norms, ones)[:live]
    next_own[live:] = lifted.astype(BF)


def pair_loop(kern_scale, pairs, count, src, tgt, wts, acc):
    last = tgt.shape[0] - 1

    def batch(i, carry):
        terms = []
        for u in range(BATCH):
            code = pairs[i * BATCH + u]
            h = code & 255
            g = code >> 8
            kernel = kernel_tile(nn_dot(tgt[jnp.minimum(g, last)], src[h]), kern_scale)
            terms.append((g, nt_dot(wts[h], kernel)))
        for g, term in terms:
            acc[g] = acc[g] + term
        return carry

    lax.fori_loop(0, (count + (BATCH - 1)) >> 3, batch, 0)


def finish_list(pairs, count, dummy):
    for u in range(BATCH):
        pairs[count + u] = dummy << 8


def near_own_kernel(kern_scale, first, near, place, src, tgt, wts, out, pairs, acc):
    targets = out.shape[0]
    leaves = src.shape[0]
    slots = near.shape[1]
    base = place[0] * leaves
    acc[...] = jnp.zeros_like(acc)
    count = jnp.int32(0)
    for t in range(targets):
        for s in range(slots):
            h = near[first + t, s] - base
            pairs[count] = h + ((first + t) << 8)
            count = count + jnp.where((h >= 0) & (h < leaves), 1, 0)
    finish_list(pairs, count, leaves)
    pair_loop(kern_scale, pairs, count, src, tgt, wts, acc)
    out[...] = acc[pl.ds(first, targets)]


def far_kernel(kern_scale, far, src, tgt, wts, out, pairs, counts, acc):
    nodes = src.shape[0]
    slots = far.shape[1]
    for i in range(nodes):
        for b in range(nodes):
            counts[i, b] = jnp.int32(1 if b == (i ^ 1) else 0)
        counts[i, nodes] = jnp.int32(0)
        for s in range(slots):
            e = far[i, s]
            at = jnp.where(e < 0, nodes, e)
            counts[i, at] = counts[i, at] + 1
    total = jnp.int32(0)
    for i in range(nodes):
        for b in range(nodes):
            pairs[total] = b + (i << 8)
            total = total + jnp.where(counts[i, b] > 0, 1, 0)
    finish_list(pairs, total, nodes)
    for b in range(nodes):
        counts[nodes, b] = jnp.int32(0)
    acc[...] = jnp.zeros_like(acc)
    last = nodes - 1

    def batch(i, carry):
        terms = []
        for u in range(BATCH):
            code = pairs[i * BATCH + u]
            h = code & 255
            g = code >> 8
            kernel = kernel_tile(nn_dot(tgt[jnp.minimum(g, last)], src[h]), kern_scale)
            times = counts[g, h].astype(F32)
            terms.append((g, nt_dot(wts[h], kernel) * times))
        for g, term in terms:
            acc[g] = acc[g] + term
        return carry

    lax.fori_loop(0, (total + (BATCH - 1)) >> 3, batch, 0)
    out[...] = acc[pl.ds(0, nodes)]


def down_kernel(
    kern_scale, upper, leaves, kernels, field1, src_up, tgt_up, wts_up, *rest
):
    chain_fields = rest[:upper]
    half_kernels = rest[upper : 2 * upper - 1]
    root, leaf_field = rest[2 * upper - 1 :]
    width = root.shape[1]
    depth = leaves.bit_length() - 1
    rhs = root.shape[0]

    def push(field, kernel):
        sums = nn_dot(with_ones(field.astype(BF)), kernel)
        return sums[:rhs] / sums[rhs : rhs + 1]

    field = chain_fields[upper - 1][...]
    for bit in range(upper - 2, -1, -1):
        field = chain_fields[bit][...] + push(field, half_kernels[bit][...])
    root[...] = field
    fields = [field]
    for height in range(depth, 0, -1):
        first_row = leaves - (leaves >> (height - 1))
        below = []
        for node in range(leaves >> height):
            pushed = push(fields[node], kernels[first_row + node])
            below += [pushed[:, :width], pushed[:, width:]]
        if height == 1:
            for leaf in range(leaves):
                leaf_field[leaf] = below[leaf]
        else:
            fields = []
            first = leaves // 2 - (leaves >> (height - 2))
            for node in range(leaves >> (height - 1)):
                if height == 2:
                    coupled = field1[node]
                else:
                    at = first + (node ^ 1)
                    kernel = kernel_tile(nn_dot(tgt_up[first + node], src_up[at]), kern_scale)
                    coupled = nt_dot(wts_up[at], kernel)
                fields.append(coupled + below[node])


def final_kernel(
    kern_scale, features, near, place, left, right, tgt, order, leaf_field, *rest
):
    *own_parts, out, src, wts, acc, pairs, spread = rest
    leaves, width, _ = tgt.shape
    slots = near.shape[1]
    rhs = out.shape[0]
    for side, halo in enumerate((left, right)):
        for leaf in range(leaves):
            cols = pl.ds(leaf * width, width)
            x = halo[:features, cols].astype(F32)
            src[side * leaves + leaf] = source_form(x, *aux_rows(x))
            wts[side * leaves + leaf] = halo[features:, cols]
    at = 0
    for part in own_parts:
        for t in range(part.shape[0]):
            acc[at] = part[t] + leaf_field[at]
            at += 1
    acc[leaves] = jnp.zeros_like(acc[leaves])
    base = place[0] * leaves

    def scan(g, count):
        for s in range(slots):
            entry = near[g, s]
            h = entry - base
            go_left = (entry >= 0) & (h < 0)
            go_right = h >= leaves
            at = jnp.where(go_right, h, h + leaves)
            pairs[count] = at + (g << 8)
            count = count + jnp.where(go_left | go_right, 1, 0)
        return count

    count = lax.fori_loop(0, leaves, scan, jnp.int32(0))
    finish_list(pairs, count, leaves)
    pair_loop(kern_scale, pairs, count, src, tgt, wts, acc)
    spread[...] = jnp.zeros_like(spread)

    def scatter(leaf, carry):
        start = pl.multiple_of(leaf * width, width)
        index = order[:, pl.ds(start, width)]
        home = index // width
        hot_t = one_hot(index & (width - 1), width)
        rows = acc[leaf]
        high = rows.astype(BF)
        low = (rows - high.astype(F32)).astype(BF)
        both = jnp.concatenate([high, low], axis=0)
        stack = []
        for b in range(leaves):
            mask = jnp.where(home == b, 1.0, 0.0).astype(BF)
            stack.append(both * mask)
        spread[...] += nt_dot(jnp.concatenate(stack, axis=0), hot_t)
        return carry

    lax.fori_loop(0, leaves, scatter, 0)
    for b in range(leaves):
        at = b * 2 * rhs
        out[:, pl.ds(b * width, width)] = spread[pl.ds(at, rhs)] + spread[pl.ds(at + rhs, rhs)]


def local(points, charges, leaf_order, near_list, far_list, local_skel, upper_skel):
    features, total = points.shape
    rhs = charges.shape[0]
    leaves, _ = near_list.shape
    width = local_skel.shape[1]
    nodes = local_skel.shape[0]
    kern_scale = 2.0 * math.sqrt(3.0 / features)
    devices = lax.axis_size("leaf")
    upper = devices.bit_length() - 1
    position = lax.axis_index("leaf")
    live = features + 2 * AUX
    rows = features + rhs
    shape = jax.ShapeDtypeStruct
    place = jnp.reshape(position, (1,)).astype(jnp.int32)

    stacked = call(
        gather_kernel,
        shape((rows, total), BF),
        [VMEM] * 3,
        [pltpu.VMEM((leaves, rows, width), BF), pltpu.VMEM((leaves, width, width), BF)],
        10**10,
    )(points, charges, leaf_order)
    ring = list(range(devices - 1))
    left = lax.ppermute(stacked, "leaf", [(i, i + 1) for i in ring])
    right = lax.ppermute(stacked, "leaf", [(i + 1, i) for i in ring])

    half, top = leaves // 2, nodes - leaves // 2
    (leaf_src, leaf_tgt, leaf_wts, src1, tgt1, wts1, src_up, tgt_up, wts_up, kernels, payload) = call(
        functools.partial(tree_kernel, kern_scale, features),
        (
            shape((leaves, DEPTH, width), BF),
            shape((leaves, width, DEPTH), BF),
            shape((leaves, rhs, width), BF),
            shape((half, DEPTH, width), BF),
            shape((half, width, DEPTH), BF),
            shape((half, rhs, width), BF),
            shape((top, DEPTH, width), BF),
            shape((top, width, DEPTH), BF),
            shape((top, rhs, width), BF),
            shape((nodes, width, 2 * width), BF),
            shape((live + rhs, width), BF),
        ),
        [VMEM] * 2,
        [pltpu.VMEM((8, DEPTH, 2 * width), BF), pltpu.VMEM((8, rhs + 16, 2 * width), BF)],
        10**10,
    )(stacked, local_skel)

    cuts = [leaves * k // (upper - 1) for k in range(upper)]
    own_parts = []
    for k in range(upper - 1):
        count = cuts[k + 1] - cuts[k]
        if count == 0:
            continue
        own_parts.append(
            call(
                functools.partial(near_own_kernel, kern_scale, cuts[k]),
                shape((count, rhs, width), F32),
                [SMEM] * 2 + [VMEM] * 3,
                [
                    pltpu.SMEM((count * near_list.shape[1] + BATCH,), jnp.int32),
                    pltpu.VMEM((leaves + 1, rhs, width), F32),
                ],
                2 * 10**9,
            )(near_list, place, leaf_src, leaf_tgt, leaf_wts)
        )
    field1 = call(
        functools.partial(far_kernel, kern_scale),
        shape((half, rhs, width), F32),
        [SMEM] + [VMEM] * 3,
        [
            pltpu.SMEM((half * half + BATCH,), jnp.int32),
            pltpu.SMEM((half + 1, half + 1), jnp.int32),
            pltpu.VMEM((half + 1, rhs, width), F32),
        ],
        4 * 10**9,
    )(far_list, src1, tgt1, wts1)

    own, own_tgt = payload, tgt_up[top - 1]
    chain_fields, half_kernels = [], []
    for bit in range(upper):
        sibling = lax.ppermute(own, "leaf", [(i, i ^ (1 << bit)) for i in range(devices)])
        if bit == upper - 1:
            chain_fields.append(
                call(
                    functools.partial(couple_kernel, kern_scale, live),
                    shape((rhs, width), F32),
                    [VMEM] * 2,
                    [],
                    10**8,
                )(sibling, own_tgt)
            )
            break
        table_row = devices - (devices >> bit) + (position >> (bit + 1))
        where = jnp.stack([table_row, (position >> bit) & 1]).astype(jnp.int32)
        field, own, own_tgt, half_kernel = call(
            functools.partial(chain_kernel, kern_scale, features),
            (
                shape((rhs, width), F32),
                shape((live + rhs, width), BF),
                shape((width, DEPTH), BF),
                shape((width, width), BF),
            ),
            [SMEM] + [VMEM] * 4,
            [pltpu.VMEM((DEPTH, 2 * width), BF), pltpu.VMEM((rhs + 16, 2 * width), BF)],
            10**8,
        )(where, own, sibling, own_tgt, upper_skel)
        chain_fields.append(field)
        half_kernels.append(half_kernel)

    root, leaf_field = call(
        functools.partial(down_kernel, kern_scale, upper, leaves),
        (shape((rhs, width), F32), shape((leaves, rhs, width), F32)),
        [VMEM] * (5 + 2 * upper - 1),
        [],
        10**9,
    )(kernels, field1, src_up, tgt_up, wts_up, *chain_fields, *half_kernels)

    potentials = call(
        functools.partial(final_kernel, kern_scale, features),
        shape((rhs, total), F32),
        [SMEM] * 2 + [VMEM] * (5 + len(own_parts)),
        [
            pltpu.VMEM((2 * leaves, DEPTH, width), BF),
            pltpu.VMEM((2 * leaves, rhs, width), BF),
            pltpu.VMEM((leaves + 1, rhs, width), F32),
            pltpu.SMEM((near_list.size + BATCH,), jnp.int32),
            pltpu.VMEM((leaves * 2 * rhs, width), F32),
        ],
        10**10,
    )(near_list, place, left, right, leaf_tgt, leaf_order, leaf_field, *own_parts)
    return (potentials, root[None])


def solution(mesh):
    placed = (
        P(None, "leaf"),
        P(None, "leaf"),
        P("leaf", None),
        P("leaf", None),
        P("leaf", None),
        P("leaf", None),
        P(),
    )
    return jax.shard_map(
        local,
        mesh=mesh,
        in_specs=placed,
        out_specs=(P(None, "leaf"), P("leaf", None, None)),
        check_vma=False,
    )
```

```python
import functools
import math

import jax
import jax.numpy as jnp
from jax import lax
from jax.experimental import pallas as pl
from jax.experimental.pallas import tpu as pltpu
from jax.sharding import PartitionSpec as P

PAIR_GAIN = math.sqrt(2.0)
LOG2E = math.log2(math.e)
BF = jnp.bfloat16
F32 = jnp.float32
NT = (((1,), (1,)), ((), ()))
AUX = 8
DEPTH = 128
BATCH, SMALL = 24, 8
FILL = 28
FILLERS = 5
UNROLL = 4
VMEM = pl.BlockSpec(memory_space=pltpu.VMEM)
SMEM = pl.BlockSpec(memory_space=pltpu.SMEM)
HBM = pl.BlockSpec(memory_space=pltpu.HBM)
ANY = pl.BlockSpec(memory_space=pl.ANY)


def nt_dot(a, b):
    return lax.dot_general(a, b, NT, preferred_element_type=F32)


def nn_dot(a, b):
    return jnp.dot(a, b, preferred_element_type=F32)


def call(body, out_shape, in_specs, scratch, flops, out_specs=None, aliases=None, limit_mb=16):
    return pl.pallas_call(
        body,
        out_shape=out_shape,
        in_specs=in_specs,
        out_specs=out_specs or jax.tree.map(lambda _: VMEM, out_shape),
        input_output_aliases=aliases or {},
        scratch_shapes=scratch,
        compiler_params=pltpu.CompilerParams(vmem_limit_bytes=limit_mb * 2**20),
        cost_estimate=pl.CostEstimate(flops=flops, bytes_accessed=2**20, transcendentals=0),
    )


def kernel_tile(sq_dist, kern_scale):
    floor = jnp.maximum(sq_dist, 1e-30)
    root = floor * lax.rsqrt(floor)
    decay = jnp.exp2(root * (-kern_scale * LOG2E))
    return ((1.0 + root * kern_scale) * decay).astype(BF)


def aux_rows(x):
    width = x.shape[1]
    norm = jnp.sum(x * x, axis=0, keepdims=True)
    high = norm.astype(BF).astype(F32)
    rest = norm - high
    mid = rest.astype(BF).astype(F32)
    low = rest - mid
    row = lax.broadcasted_iota(jnp.int32, (AUX, width), 0)
    norms = jnp.where(row == 0, high, jnp.where(row == 1, mid, jnp.where(row == 2, low, 0.0)))
    ones = jnp.where(row < 3, 1.0, 0.0)
    return norms, ones


def source_form(x, norms, ones):
    pad = jnp.zeros((DEPTH - x.shape[0] - 2 * AUX, x.shape[1]), F32)
    return jnp.concatenate([x, norms, ones, pad], axis=0).astype(BF)


def target_form(x, norms, ones):
    pad = jnp.zeros((DEPTH - x.shape[0] - 2 * AUX, x.shape[1]), F32)
    return jnp.concatenate([-2.0 * x, ones, norms, pad], axis=0).T.astype(BF)


def split_form(selected, features):
    return (
        selected[:features],
        selected[features : features + AUX],
        selected[features + AUX : features + 2 * AUX],
    )


def one_hot(chosen, height):
    width = chosen.shape[1]
    row = lax.broadcasted_iota(jnp.int32, (height, width), 0)
    return jnp.where(row == chosen, 1.0, 0.0).astype(BF)


def flat(table, size):
    rows, cols = table.shape
    entry = lax.broadcasted_iota(jnp.int32, (cols, size), 1)
    pick = jnp.where(entry % cols == lax.broadcasted_iota(jnp.int32, (cols, size), 0), 1.0, 0.0)
    every = nn_dot(table.astype(BF), pick.astype(BF))
    entry = lax.broadcasted_iota(jnp.int32, (rows, size), 1)
    row = lax.broadcasted_iota(jnp.int32, (rows, size), 0)
    return jnp.sum(jnp.where(entry // cols == row, every, 0.0), axis=0, keepdims=True)


def pair_list(near, far, first_leaf, length, fixed):
    leaves, slots = near.shape
    nodes, _ = far.shape
    upper = nodes - 2
    near_size, far_size = leaves * slots, nodes * nodes
    size = -(-(near_size + far_size + upper) // 128) * 128
    rest = size - near_size - far_size
    row = lax.broadcasted_iota(jnp.int32, (nodes, nodes), 0)
    col = lax.broadcasted_iota(jnp.int32, (nodes, nodes), 1)
    seen = jnp.where(col == row + 1 - 2 * (row & 1), 1.0, 0.0)
    for s in range(far.shape[1]):
        seen = seen + jnp.where(far[:, s : s + 1] == col, 1.0, 0.0)
    here = jnp.where(near >= 0, near - (first_leaf - leaves), -1).astype(F32)
    column = lax.broadcasted_iota(jnp.int32, (1, size), 1)
    is_far = (column >= near_size) & (column < near_size + far_size)
    is_up = (column >= near_size + far_size) & (column < near_size + far_size + upper)
    near_h = jnp.concatenate([flat(here, near_size), jnp.full((1, size - near_size), -1.0, F32)], axis=1)
    times = jnp.concatenate(
        [jnp.zeros((1, near_size), F32), flat(seen, far_size + rest)], axis=1
    )
    from_far = column - near_size
    from_up = from_far - far_size
    node_first = 2 * leaves
    up_at = nodes + from_up
    sibling = up_at + 1 - 2 * (from_up & 1)
    source = jnp.where(
        is_far, node_first + from_far % nodes, jnp.where(is_up, node_first + sibling, 0)
    ).astype(F32) + jnp.where(column < near_size, near_h, 0.0)
    target = jnp.where(
        is_far, leaves + from_far // nodes, jnp.where(is_up, leaves + up_at, column // slots)
    ).astype(F32)
    times = jnp.where(is_far, times, jnp.where(is_up | (near_h >= 0), 1.0, 0.0))
    level = jnp.where(times > 0, 1.0, 0.0)
    first = jnp.where(is_far | is_up, level, 0.0)
    own = jnp.where((near_h >= leaves) & (near_h < 2 * leaves), 1.0, 0.0)
    other = level - first - own
    row = lax.broadcasted_iota(jnp.int32, (16, size), 0)
    masks = jnp.where(row == 0, first, jnp.where(row == 1, own, jnp.where(row == 2, other, 0.0)))
    before = lax.broadcasted_iota(jnp.int32, (size, size), 1) < lax.broadcasted_iota(
        jnp.int32, (size, size), 0
    )
    rank = nt_dot(masks.astype(BF), jnp.where(before, 1.0, 0.0).astype(BF))
    found = jnp.sum(masks, axis=1, keepdims=True)
    start = jnp.maximum(found[0:1] + found[1:2], float(fixed))
    place = jnp.where(other > 0, start + rank[2:3], -1.0)
    place = jnp.where(own > 0, found[0:1] + rank[1:2], place)
    place = jnp.where(first > 0, rank[0:1], place)
    slot = lax.broadcasted_iota(jnp.int32, (length, size), 0).astype(F32)
    hit = jnp.where(slot == place, 1.0, 0.0).astype(BF)
    parts = jnp.where(row == 0, source, jnp.where(row == 1, target, jnp.where(row == 2, times, 0.0)))
    listed = nt_dot(parts.astype(BF), hit)
    code = (listed[0:1] + 256.0 * listed[1:2] + 65536.0 * listed[2:3]).astype(jnp.int32)
    code = jnp.where(listed[2:3] > 0.5, code, leaves)
    total = jnp.broadcast_to(start + found[2:3], (1, length)).astype(jnp.int32)
    return jnp.concatenate([code, total], axis=0)


def gather_kernel(
    fixed, points, charges, order, near, far, place, stacked, pairs, grid, hots, index, slots, far_slots, sems
):
    features, total = points.shape
    rows = stacked.shape[0]
    width = hots.shape[1]
    blocks = grid.shape[0]
    fetch_index = pltpu.make_async_copy(order, index, sems.at[2 * blocks])
    fetch_index.start()
    fetches = []
    for b in range(blocks):
        cols = pl.ds(b * width, width)
        into = grid.at[b, pl.ds(0, features)]
        fetches.append(pltpu.make_async_copy(points.at[:, cols], into, sems.at[2 * b]))
        into = grid.at[b, pl.ds(features, rows - features)]
        fetches.append(pltpu.make_async_copy(charges.at[:, cols], into, sems.at[2 * b + 1]))
    fetch_slots = pltpu.make_async_copy(near, slots, sems.at[2 * blocks + 1])
    fetch_slots.start()
    fetch_far = pltpu.make_async_copy(far, far_slots, sems.at[2 * blocks + 2])
    fetch_far.start()
    for fetch in fetches:
        fetch.start()
    fetch_index.wait()
    for b in range(blocks):
        hots[b] = one_hot(index[:, pl.ds(b * width, width)] & (width - 1), width)
    fetch_slots.wait()
    fetch_far.wait()
    pairs[...] = pair_list(slots[...], far_slots[...], place[0] * blocks, pairs.shape[1], fixed)
    for fetch in fetches:
        fetch.wait()

    def block(i, carry):
        for u in range(UNROLL):
            j = i * UNROLL + u
            start = pl.multiple_of(j * width, width)
            home = index[:, pl.ds(start, width)] // width
            spread = nn_dot(grid[...].reshape(blocks * rows, width), hots[j])
            found = spread[:rows]
            for b in range(1, blocks):
                found = jnp.where(home == b, spread[b * rows : (b + 1) * rows], found)
            stacked[:, pl.ds(start, width)] = found.astype(BF)
        return carry

    lax.fori_loop(0, blocks // UNROLL, block, 0)


def lift(sources, weights, target, kern_scale):
    kernel = kernel_tile(nn_dot(target, sources), kern_scale)
    sums = nt_dot(weights, kernel)
    rhs = weights.shape[0] - 16
    lifted = PAIR_GAIN * (sums[:rhs] / sums[rhs : rhs + 1])
    return kernel, lifted


def with_ones(weights):
    return jnp.concatenate([weights, jnp.ones((16, weights.shape[1]), weights.dtype)], axis=0)


def tree_kernel(
    kern_scale, features, stacked, skel, srcs, tgts, wtss, kernels, payload, top_tgt, joined, joined_w,
):
    width = skel.shape[1]
    nodes = skel.shape[0]
    leaves = nodes + 1
    for leaf in range(leaves):
        cols = pl.ds(leaf * width, width)
        x = stacked[:features, cols].astype(F32)
        norms, ones = aux_rows(x)
        srcs[leaf] = source_form(x, norms, ones)
        tgts[leaf] = target_form(x, norms, ones)
        wtss[leaf] = stacked[features:, cols]
    live = features + 2 * AUX
    for row in range(nodes):
        slot = row % 8
        for side in range(2):
            joined[slot, :, side * width : (side + 1) * width] = srcs[2 * row + side]
            joined_w[slot, :, side * width : (side + 1) * width] = with_ones(wtss[2 * row + side])
        hot = one_hot(skel[row : row + 1, :], 2 * width)
        x, norms, ones = split_form(nn_dot(joined[slot, :live], hot), features)
        own_src = source_form(x, norms, ones)
        own_tgt = target_form(x, norms, ones)
        kernel, lifted = lift(joined[slot], joined_w[slot], own_tgt, kern_scale)
        kernels[row] = kernel
        own_wts = lifted.astype(BF)
        if row < nodes - 1:
            srcs[leaves + row], tgts[leaves + row], wtss[leaves + row] = own_src, own_tgt, own_wts
        else:
            payload[:live] = own_src[:live]
            payload[live:] = own_wts
            top_tgt[...] = own_tgt


def padded(rows):
    return jnp.concatenate(
        [rows, jnp.zeros((DEPTH - rows.shape[0], rows.shape[1]), rows.dtype)], axis=0
    )


def chain_kernel(
    kern_scale, features, bit, devices, place, own, sibling, skel, _, next_own, next_tgt, half_kernel, joined, joined_w
):
    live = features + 2 * AUX
    width = own.shape[1]
    joined[:, :width] = padded(own[:live])
    joined[:, width:] = padded(sibling[:live])
    joined_w[:, :width] = with_ones(own[live:])
    joined_w[:, width:] = with_ones(sibling[live:])
    chosen = skel[pl.ds(devices - (devices >> bit) + (place[0] >> (bit + 1)), 1), :]
    chosen = chosen + ((place[0] >> bit) & 1) * jnp.where(chosen < width, width, -width)
    hot = one_hot(chosen, 2 * width)
    x, norms, ones = split_form(nn_dot(joined[:live], hot), features)
    target = target_form(x, norms, ones)
    kernel, lifted = lift(joined[...], joined_w[...], target, kern_scale)
    half_kernel[...] = kernel[:, :width]
    next_tgt[...] = target
    next_own[:live] = source_form(x, norms, ones)[:live]
    next_own[live:] = lifted.astype(BF)


def pair_terms(kern_scale, codes, src, tgt, wts, acc, first=0):
    terms = []
    for code in codes:
        h = (code & 255) - first
        g = (code >> 8) & 255
        times = (code >> 16).astype(F32)
        kernel = kernel_tile(nn_dot(tgt[g], src[h]), kern_scale)
        terms.append((g, nt_dot(wts[h], kernel) * times))
    for g, term in terms:
        acc[g] = acc[g] + term


def pair_loop(total, batch):
    large = total // BATCH

    def step(i, carry):
        batch(i * BATCH, BATCH)
        return carry

    def small_step(i, carry):
        batch(large * BATCH + i * SMALL, SMALL)
        return carry

    lax.fori_loop(0, large, step, 0)
    lax.fori_loop(0, (total - large * BATCH + (SMALL - 1)) // SMALL, small_step, 0)


def own_kernel(kern_scale, part, pairs, src, tgt, wts, _, *rest):
    acc = rest[-1]
    if part == 0:
        acc[...] = jnp.zeros_like(acc)
    codes = [pairs[0, part * FILL + u] for u in range(FILL)]
    pair_terms(kern_scale, codes, src, tgt, wts, acc, (src.shape[0] + 2) // 2)


def down_kernel(kern_scale, upper, live, kernels, acc, *rest):
    siblings = rest[:upper]
    targets = rest[upper : 2 * upper]
    half_kernels = rest[2 * upper : 3 * upper - 1]
    root, leaf_field = rest[3 * upper - 1 :]
    width = root.shape[1]
    nodes = kernels.shape[0]
    leaves = nodes + 1
    rhs = root.shape[0]

    def push(field, kernel):
        sums = nn_dot(with_ones(field.astype(BF)), kernel)
        return sums[:rhs] / sums[rhs : rhs + 1]

    coupled = []
    for bit in range(upper):
        kernel = kernel_tile(nn_dot(targets[bit][...], padded(siblings[bit][:live])), kern_scale)
        coupled.append(nt_dot(siblings[bit][live:], kernel))
    field = coupled[upper - 1]
    for bit in range(upper - 2, -1, -1):
        field = coupled[bit] + push(field, half_kernels[bit][...])
    root[...] = field
    fields = {nodes - 1: field}
    for row in range(nodes - 1, -1, -1):
        pushed = push(fields[row], kernels[row])
        for side in range(2):
            below = 2 * row + side
            passed = pushed[:, side * width : (side + 1) * width]
            if below < leaves:
                leaf_field[below] = passed
            else:
                fields[below - leaves] = acc[below] + passed


def final_kernel(
    kern_scale, features, fixed, pairs, left, right, own_src, own_wts, tgt, order, leaf_field, own_acc,
    out, src, wts, acc, spread,
):
    leaves = leaf_field.shape[0]
    width = leaf_field.shape[2]
    rhs = out.shape[0]
    for side, halo in ((0, left), (2, right)):
        for leaf in range(leaves):
            cols = pl.ds(leaf * width, width)
            x = halo[:features, cols].astype(F32)
            src[side * leaves + leaf] = source_form(x, *aux_rows(x))
            wts[side * leaves + leaf] = halo[features:, cols]
    src[pl.ds(leaves, leaves)] = own_src[pl.ds(0, leaves)]
    wts[pl.ds(leaves, leaves)] = own_wts[pl.ds(0, leaves)]
    acc[...] = own_acc[pl.ds(0, leaves)] + leaf_field[...]

    def batch(first, size):
        codes = [pairs[0, fixed + first + u] for u in range(size)]
        pair_terms(kern_scale, codes, src, tgt, wts, acc)

    pair_loop(pairs[1, 0] - fixed, batch)
    spread[...] = jnp.zeros_like(spread)
    span = UNROLL * width

    def scatter(i, carry):
        index = order[:, pl.ds(pl.multiple_of(i * span, span), span)]
        home = index // width
        hot_t = one_hot(index & (width - 1), width)
        rows = jnp.concatenate([acc[i * UNROLL + u] for u in range(UNROLL)], axis=1)
        high = rows.astype(BF)
        low = (rows - high.astype(F32)).astype(BF)
        both = jnp.concatenate([high, low], axis=0)
        stack = []
        for b in range(leaves):
            mask = jnp.where(home == b, 1.0, 0.0).astype(BF)
            stack.append(both * mask)
        spread[...] += nt_dot(jnp.concatenate(stack, axis=0), hot_t)
        return carry

    lax.fori_loop(0, leaves // UNROLL, scatter, 0)
    for b in range(leaves):
        at = b * 2 * rhs
        out[:, pl.ds(b * width, width)] = spread[pl.ds(at, rhs)] + spread[pl.ds(at + rhs, rhs)]


def local(points, charges, leaf_order, near_list, far_list, local_skel, upper_skel):
    features, total = points.shape
    rhs = charges.shape[0]
    leaves, _ = near_list.shape
    width = local_skel.shape[1]
    nodes = local_skel.shape[0]
    kern_scale = 2.0 * math.sqrt(3.0 / features)
    devices = lax.axis_size("leaf")
    upper = devices.bit_length() - 1
    depth = leaves.bit_length() - 1
    position = lax.axis_index("leaf")
    live = features + 2 * AUX
    rows = features + rhs
    shape = jax.ShapeDtypeStruct
    place = jnp.reshape(position, (1,)).astype(jnp.int32)

    half = leaves // 2
    fillers = min(FILLERS, upper)
    fixed = fillers * FILL
    pairs_most = near_list.size + half * half + half - 2
    length = -(-(max(pairs_most, near_list.size + fixed) + BATCH) // 128) * 128
    stacked, pairs = call(
        functools.partial(gather_kernel, fixed),
        (shape((rows, total), BF), shape((2, length), jnp.int32)),
        [HBM] * 5 + [SMEM],
        [
            pltpu.VMEM((leaves, rows, width), BF),
            pltpu.VMEM((leaves, width, width), BF),
            pltpu.VMEM((1, total), jnp.int32),
            pltpu.VMEM(near_list.shape, jnp.int32),
            pltpu.VMEM(far_list.shape, jnp.int32),
            pltpu.SemaphoreType.DMA((2 * leaves + 3,)),
        ],
        10**10,
        limit_mb=63,
    )(points, charges, leaf_order, near_list, far_list, place)
    ring = list(range(devices - 1))
    left = lax.ppermute(stacked, "leaf", [(i, i + 1) for i in ring])
    right = lax.ppermute(stacked, "leaf", [(i + 1, i) for i in ring])

    known = leaves + nodes - 1
    srcs, tgts, wtss, kernels, own, own_tgt = call(
        functools.partial(tree_kernel, kern_scale, features),
        (
            shape((known, DEPTH, width), BF),
            shape((known, width, DEPTH), BF),
            shape((known, rhs, width), BF),
            shape((nodes, width, 2 * width), BF),
            shape((live + rhs, width), BF),
            shape((width, DEPTH), BF),
        ),
        [VMEM] * 2,
        [pltpu.VMEM((8, DEPTH, 2 * width), BF), pltpu.VMEM((8, rhs + 16, 2 * width), BF)],
        10**10,
    )(stacked, local_skel)

    siblings, targets, half_kernels = [], [], []
    acc = None
    for bit in range(upper):
        sibling = lax.ppermute(own, "leaf", [(i, i ^ (1 << bit)) for i in range(devices)])
        if bit < fillers:
            acc = call(
                functools.partial(own_kernel, kern_scale, bit),
                shape((known, rhs, width), F32),
                [SMEM] + [VMEM] * 3 + [ANY] + [VMEM] * (bit > 0),
                [],
                4 * 10**9,
                aliases={5: 0} if bit else None,
            )(pairs, srcs, tgts, wtss, own, *([acc] if bit else []))
        siblings.append(sibling)
        targets.append(own_tgt)
        if bit == upper - 1:
            break
        own, own_tgt, half_kernel = call(
            functools.partial(chain_kernel, kern_scale, features, bit, devices),
            (
                shape((live + rhs, width), BF),
                shape((width, DEPTH), BF),
                shape((width, width), BF),
            ),
            [SMEM] + [VMEM] * 3 + [ANY],
            [pltpu.VMEM((DEPTH, 2 * width), BF), pltpu.VMEM((rhs + 16, 2 * width), BF)],
            10**8,
        )(place, own, sibling, upper_skel, acc)
        half_kernels.append(half_kernel)

    root, leaf_field = call(
        functools.partial(down_kernel, kern_scale, upper, live),
        (shape((rhs, width), F32), shape((leaves, rhs, width), F32)),
        [VMEM] * (2 + 3 * upper - 1),
        [],
        10**9,
    )(kernels, acc, *siblings, *targets, *half_kernels)

    potentials = call(
        functools.partial(final_kernel, kern_scale, features, fixed),
        shape((rhs, total), F32),
        [SMEM] + [VMEM] * 8,
        [
            pltpu.VMEM((3 * leaves, DEPTH, width), BF),
            pltpu.VMEM((3 * leaves, rhs, width), BF),
            pltpu.VMEM((leaves, rhs, width), F32),
            pltpu.VMEM((leaves * 2 * rhs, width), F32),
        ],
        10**10,
    )(pairs, left, right, srcs, wtss, tgts, leaf_order, leaf_field, acc)
    return (potentials, root[None])


def solution(mesh):
    placed = (
        P(None, "leaf"),
        P(None, "leaf"),
        P("leaf", None),
        P("leaf", None),
        P("leaf", None),
        P("leaf", None),
        P(),
    )
    return jax.shard_map(
        local,
        mesh=mesh,
        in_specs=placed,
        out_specs=(P(None, "leaf"), P("leaf", None, None)),
        check_vma=False,
    )
```

```python
import functools
import math

import jax
import jax.numpy as jnp
from jax import lax
from jax.experimental import pallas as pl
from jax.experimental.pallas import tpu as pltpu
from jax.sharding import PartitionSpec as P

PAIR_GAIN = math.sqrt(2.0)
LOG2E = math.log2(math.e)
BF = jnp.bfloat16
F32 = jnp.float32
NT = (((1,), (1,)), ((), ()))
AUX = 8
DEPTH = 128
BATCH, SMALL = 24, 8
OWN_PARTS = (72, 72)
ANY_PARTS = (28, 36, 36)
UNROLL = 4
VMEM = pl.BlockSpec(memory_space=pltpu.VMEM)
SMEM = pl.BlockSpec(memory_space=pltpu.SMEM)
HBM = pl.BlockSpec(memory_space=pltpu.HBM)
ANY = pl.BlockSpec(memory_space=pl.ANY)


def nt_dot(a, b):
    return lax.dot_general(a, b, NT, preferred_element_type=F32)


def nn_dot(a, b):
    return jnp.dot(a, b, preferred_element_type=F32)


def call(body, out_shape, in_specs, scratch, flops, out_specs=None, aliases=None, limit_mb=16):
    return pl.pallas_call(
        body,
        out_shape=out_shape,
        in_specs=in_specs,
        out_specs=out_specs or jax.tree.map(lambda _: VMEM, out_shape),
        input_output_aliases=aliases or {},
        scratch_shapes=scratch,
        compiler_params=pltpu.CompilerParams(vmem_limit_bytes=limit_mb * 2**20),
        cost_estimate=pl.CostEstimate(flops=flops, bytes_accessed=2**20, transcendentals=0),
    )


def kernel_tile(sq_dist, kern_scale):
    floor = jnp.maximum(sq_dist, 1e-30)
    root = floor * lax.rsqrt(floor)
    decay = jnp.exp2(root * (-kern_scale * LOG2E))
    return ((1.0 + root * kern_scale) * decay).astype(BF)


def aux_rows(x):
    width = x.shape[1]
    norm = jnp.sum(x * x, axis=0, keepdims=True)
    high = norm.astype(BF).astype(F32)
    rest = norm - high
    mid = rest.astype(BF).astype(F32)
    low = rest - mid
    row = lax.broadcasted_iota(jnp.int32, (AUX, width), 0)
    norms = jnp.where(row == 0, high, jnp.where(row == 1, mid, jnp.where(row == 2, low, 0.0)))
    ones = jnp.where(row < 3, 1.0, 0.0)
    return norms, ones


def source_form(x, norms, ones):
    pad = jnp.zeros((DEPTH - x.shape[0] - 2 * AUX, x.shape[1]), F32)
    return jnp.concatenate([x, norms, ones, pad], axis=0).astype(BF)


def target_form(x, norms, ones):
    pad = jnp.zeros((DEPTH - x.shape[0] - 2 * AUX, x.shape[1]), F32)
    return jnp.concatenate([-2.0 * x, ones, norms, pad], axis=0).T.astype(BF)


def split_form(selected, features):
    return (
        selected[:features],
        selected[features : features + AUX],
        selected[features + AUX : features + 2 * AUX],
    )


def one_hot(chosen, height):
    width = chosen.shape[1]
    row = lax.broadcasted_iota(jnp.int32, (height, width), 0)
    return jnp.where(row == chosen, 1.0, 0.0).astype(BF)


def flat(table, size):
    rows, cols = table.shape
    entry = lax.broadcasted_iota(jnp.int32, (cols, size), 1)
    pick = jnp.where(entry % cols == lax.broadcasted_iota(jnp.int32, (cols, size), 0), 1.0, 0.0)
    every = nn_dot(table.astype(BF), pick.astype(BF))
    entry = lax.broadcasted_iota(jnp.int32, (rows, size), 1)
    row = lax.broadcasted_iota(jnp.int32, (rows, size), 0)
    return jnp.sum(jnp.where(entry // cols == row, every, 0.0), axis=0, keepdims=True)


def pair_list(near, far, first_leaf, length, fixed):
    leaves, slots = near.shape
    nodes, _ = far.shape
    upper = nodes - 2
    near_size, far_size = leaves * slots, nodes * nodes
    size = -(-(near_size + far_size + upper) // 128) * 128
    rest = size - near_size - far_size
    row = lax.broadcasted_iota(jnp.int32, (nodes, nodes), 0)
    col = lax.broadcasted_iota(jnp.int32, (nodes, nodes), 1)
    seen = jnp.where(col == row + 1 - 2 * (row & 1), 1.0, 0.0)
    for s in range(far.shape[1]):
        seen = seen + jnp.where(far[:, s : s + 1] == col, 1.0, 0.0)
    here = jnp.where(near >= 0, near - (first_leaf - leaves), -1).astype(F32)
    column = lax.broadcasted_iota(jnp.int32, (1, size), 1)
    is_far = (column >= near_size) & (column < near_size + far_size)
    is_up = (column >= near_size + far_size) & (column < near_size + far_size + upper)
    near_h = jnp.concatenate([flat(here, near_size), jnp.full((1, size - near_size), -1.0, F32)], axis=1)
    times = jnp.concatenate(
        [jnp.zeros((1, near_size), F32), flat(seen, far_size + rest)], axis=1
    )
    from_far = column - near_size
    from_up = from_far - far_size
    node_first = 2 * leaves
    up_at = nodes + from_up
    sibling = up_at + 1 - 2 * (from_up & 1)
    source = jnp.where(
        is_far, node_first + from_far % nodes, jnp.where(is_up, node_first + sibling, 0)
    ).astype(F32) + jnp.where(column < near_size, near_h, 0.0)
    target = jnp.where(
        is_far, leaves + from_far // nodes, jnp.where(is_up, leaves + up_at, column // slots)
    ).astype(F32)
    times = jnp.where(is_far, times, jnp.where(is_up | (near_h >= 0), 1.0, 0.0))
    level = jnp.where(times > 0, 1.0, 0.0)
    first = jnp.where(is_far | is_up, level, 0.0)
    own = jnp.where((near_h >= leaves) & (near_h < 2 * leaves), 1.0, 0.0)
    other = level - first - own
    row = lax.broadcasted_iota(jnp.int32, (16, size), 0)
    masks = jnp.where(row == 0, first, jnp.where(row == 1, own, jnp.where(row == 2, other, 0.0)))
    before = lax.broadcasted_iota(jnp.int32, (size, size), 1) < lax.broadcasted_iota(
        jnp.int32, (size, size), 0
    )
    rank = nt_dot(masks.astype(BF), jnp.where(before, 1.0, 0.0).astype(BF))
    found = jnp.sum(masks, axis=1, keepdims=True)
    start = jnp.maximum(found[0:1] + found[1:2], float(fixed))
    place = jnp.where(other > 0, start + rank[2:3], -1.0)
    place = jnp.where(own > 0, found[0:1] + rank[1:2], place)
    place = jnp.where(first > 0, rank[0:1], place)
    slot = lax.broadcasted_iota(jnp.int32, (length, size), 0).astype(F32)
    hit = jnp.where(slot == place, 1.0, 0.0).astype(BF)
    parts = jnp.where(row == 0, source, jnp.where(row == 1, target, jnp.where(row == 2, times, 0.0)))
    listed = nt_dot(parts.astype(BF), hit)
    code = (listed[0:1] + 256.0 * listed[1:2] + 65536.0 * listed[2:3]).astype(jnp.int32)
    code = jnp.where(listed[2:3] > 0.5, code, leaves)
    total = jnp.broadcast_to(start + found[2:3], (1, length)).astype(jnp.int32)
    return jnp.concatenate([code, total], axis=0)


def gather_kernel(
    fixed, points, charges, order, near, far, place, stacked, pairs, grid, hots, index, slots, far_slots, sems
):
    features, total = points.shape
    rows = stacked.shape[0]
    width = hots.shape[1]
    blocks = grid.shape[0]
    fetch_index = pltpu.make_async_copy(order, index, sems.at[2 * blocks])
    fetch_index.start()
    fetches = []
    for b in range(blocks):
        cols = pl.ds(b * width, width)
        into = grid.at[b, pl.ds(0, features)]
        fetches.append(pltpu.make_async_copy(points.at[:, cols], into, sems.at[2 * b]))
        into = grid.at[b, pl.ds(features, rows - features)]
        fetches.append(pltpu.make_async_copy(charges.at[:, cols], into, sems.at[2 * b + 1]))
    fetch_slots = pltpu.make_async_copy(near, slots, sems.at[2 * blocks + 1])
    fetch_slots.start()
    fetch_far = pltpu.make_async_copy(far, far_slots, sems.at[2 * blocks + 2])
    fetch_far.start()
    for fetch in fetches:
        fetch.start()
    fetch_index.wait()
    for b in range(blocks):
        hots[b] = one_hot(index[:, pl.ds(b * width, width)] & (width - 1), width)
    fetch_slots.wait()
    fetch_far.wait()
    pairs[...] = pair_list(slots[...], far_slots[...], place[0] * blocks, pairs.shape[1], fixed)
    for fetch in fetches:
        fetch.wait()

    def block(i, carry):
        for u in range(UNROLL):
            j = i * UNROLL + u
            start = pl.multiple_of(j * width, width)
            home = index[:, pl.ds(start, width)] // width
            spread = nn_dot(grid[...].reshape(blocks * rows, width), hots[j])
            found = spread[:rows]
            for b in range(1, blocks):
                found = jnp.where(home == b, spread[b * rows : (b + 1) * rows], found)
            stacked[:, pl.ds(start, width)] = found.astype(BF)
        return carry

    lax.fori_loop(0, blocks // UNROLL, block, 0)


def lift(sources, weights, target, kern_scale):
    kernel = kernel_tile(nn_dot(target, sources), kern_scale)
    sums = nt_dot(weights, kernel)
    rhs = weights.shape[0] - 16
    lifted = PAIR_GAIN * (sums[:rhs] / sums[rhs : rhs + 1])
    return kernel, lifted


def with_ones(weights):
    return jnp.concatenate([weights, jnp.ones((16, weights.shape[1]), weights.dtype)], axis=0)


def tree_kernel(
    kern_scale, features, stacked, skel, srcs, tgts, wtss, kernels, payload, top_tgt, joined, joined_w,
):
    width = skel.shape[1]
    nodes = skel.shape[0]
    leaves = nodes + 1
    for leaf in range(leaves):
        cols = pl.ds(leaf * width, width)
        x = stacked[:features, cols].astype(F32)
        norms, ones = aux_rows(x)
        srcs[leaf] = source_form(x, norms, ones)
        tgts[leaf] = target_form(x, norms, ones)
        wtss[leaf] = stacked[features:, cols]
    live = features + 2 * AUX
    for row in range(nodes):
        slot = row % 8
        for side in range(2):
            joined[slot, :, side * width : (side + 1) * width] = srcs[2 * row + side]
            joined_w[slot, :, side * width : (side + 1) * width] = with_ones(wtss[2 * row + side])
        hot = one_hot(skel[row : row + 1, :], 2 * width)
        x, norms, ones = split_form(nn_dot(joined[slot, :live], hot), features)
        own_src = source_form(x, norms, ones)
        own_tgt = target_form(x, norms, ones)
        kernel, lifted = lift(joined[slot], joined_w[slot], own_tgt, kern_scale)
        kernels[row] = kernel
        own_wts = lifted.astype(BF)
        if row < nodes - 1:
            srcs[leaves + row], tgts[leaves + row], wtss[leaves + row] = own_src, own_tgt, own_wts
        else:
            payload[:live] = own_src[:live]
            payload[live:] = own_wts
            top_tgt[...] = own_tgt


def padded(rows):
    return jnp.concatenate(
        [rows, jnp.zeros((DEPTH - rows.shape[0], rows.shape[1]), rows.dtype)], axis=0
    )


def chain_kernel(
    kern_scale, features, bit, devices, place, own, sibling, skel, _, next_own, next_tgt, half_kernel, joined, joined_w
):
    live = features + 2 * AUX
    width = own.shape[1]
    joined[:, :width] = padded(own[:live])
    joined[:, width:] = padded(sibling[:live])
    joined_w[:, :width] = with_ones(own[live:])
    joined_w[:, width:] = with_ones(sibling[live:])
    chosen = skel[pl.ds(devices - (devices >> bit) + (place[0] >> (bit + 1)), 1), :]
    chosen = chosen + ((place[0] >> bit) & 1) * jnp.where(chosen < width, width, -width)
    hot = one_hot(chosen, 2 * width)
    x, norms, ones = split_form(nn_dot(joined[:live], hot), features)
    target = target_form(x, norms, ones)
    kernel, lifted = lift(joined[...], joined_w[...], target, kern_scale)
    half_kernel[...] = kernel[:, :width]
    next_tgt[...] = target
    next_own[:live] = source_form(x, norms, ones)[:live]
    next_own[live:] = lifted.astype(BF)


def pair_terms(kern_scale, codes, src, tgt, wts, acc, first=0):
    terms = []
    for code in codes:
        h = (code & 255) - first
        g = (code >> 8) & 255
        times = (code >> 16).astype(F32)
        kernel = kernel_tile(nn_dot(tgt[g], src[h]), kern_scale)
        terms.append((g, nt_dot(wts[h], kernel) * times))
    for g, term in terms:
        acc[g] = acc[g] + term


def pair_loop(total, batch):
    large = total // BATCH

    def step(i, carry):
        batch(i * BATCH, BATCH)
        return carry

    def small_step(i, carry):
        batch(large * BATCH + i * SMALL, SMALL)
        return carry

    lax.fori_loop(0, large, step, 0)
    lax.fori_loop(0, (total - large * BATCH + (SMALL - 1)) // SMALL, small_step, 0)


def fixed_pairs(kern_scale, start, count, pairs, src, tgt, wts, acc, first=0):
    def step(i, carry):
        codes = [pairs[0, start + i * size + u] for u in range(size)]
        pair_terms(kern_scale, codes, src, tgt, wts, acc, first)
        return carry

    size = count if count <= 36 else BATCH
    lax.fori_loop(0, count // size, step, 0)


def own_kernel(kern_scale, start, count, pairs, src, tgt, wts, _, *rest):
    acc = rest[-1]
    if start == 0:
        acc[...] = jnp.zeros_like(acc)
    fixed_pairs(kern_scale, start, count, pairs, src, tgt, wts, acc, (src.shape[0] + 2) // 2)


def meet_kernel(
    kern_scale, features, start, count, pairs, place, within, across, own_src, tgt, own_wts, _, _acc,
    acc, src, wts,
):
    leaves = src.shape[0] // 3
    width = src.shape[2]
    odd = place[0] & 1
    for halo, side in ((within, 2 - 2 * odd), (across, 2 * odd)):
        for leaf in range(leaves):
            cols = pl.ds(leaf * width, width)
            x = halo[:features, cols].astype(F32)
            at = side * leaves + leaf
            src[at] = source_form(x, *aux_rows(x))
            wts[at] = halo[features:, cols]
    src[pl.ds(leaves, leaves)] = own_src[pl.ds(0, leaves)]
    wts[pl.ds(leaves, leaves)] = own_wts[pl.ds(0, leaves)]
    fixed_pairs(kern_scale, start, count, pairs, src, tgt, wts, acc)


def any_kernel(kern_scale, start, count, pairs, src, tgt, wts, _, _acc, acc):
    fixed_pairs(kern_scale, start, count, pairs, src, tgt, wts, acc)


def down_kernel(kern_scale, upper, live, kernels, acc, *rest):
    siblings = rest[:upper]
    targets = rest[upper : 2 * upper]
    half_kernels = rest[2 * upper : 3 * upper - 1]
    root, leaf_field = rest[3 * upper - 1 :]
    width = root.shape[1]
    nodes = kernels.shape[0]
    leaves = nodes + 1
    rhs = root.shape[0]

    def push(field, kernel):
        sums = nn_dot(with_ones(field.astype(BF)), kernel)
        return sums[:rhs] / sums[rhs : rhs + 1]

    coupled = []
    for bit in range(upper):
        kernel = kernel_tile(nn_dot(targets[bit][...], padded(siblings[bit][:live])), kern_scale)
        coupled.append(nt_dot(siblings[bit][live:], kernel))
    field = coupled[upper - 1]
    for bit in range(upper - 2, -1, -1):
        field = coupled[bit] + push(field, half_kernels[bit][...])
    root[...] = field
    fields = {nodes - 1: field}
    for row in range(nodes - 1, -1, -1):
        pushed = push(fields[row], kernels[row])
        for side in range(2):
            below = 2 * row + side
            passed = pushed[:, side * width : (side + 1) * width]
            if below < leaves:
                leaf_field[below] = passed
            else:
                fields[below - leaves] = acc[below] + passed


def final_kernel(
    kern_scale, fixed, pairs, src, tgt, wts, order, leaf_field, all_acc, out, acc, spread
):
    leaves = leaf_field.shape[0]
    width = leaf_field.shape[2]
    rhs = out.shape[0]
    acc[...] = all_acc[pl.ds(0, leaves)] + leaf_field[...]

    def batch(first, size):
        codes = [pairs[0, fixed + first + u] for u in range(size)]
        pair_terms(kern_scale, codes, src, tgt, wts, acc)

    pair_loop(jnp.maximum(pairs[1, 0] - fixed, 0), batch)
    spread[...] = jnp.zeros_like(spread)
    span = UNROLL * width

    def scatter(i, carry):
        index = order[:, pl.ds(pl.multiple_of(i * span, span), span)]
        home = index // width
        hot_t = one_hot(index & (width - 1), width)
        rows = jnp.concatenate([acc[i * UNROLL + u] for u in range(UNROLL)], axis=1)
        high = rows.astype(BF)
        low = (rows - high.astype(F32)).astype(BF)
        both = jnp.concatenate([high, low], axis=0)
        stack = []
        for b in range(leaves):
            mask = jnp.where(home == b, 1.0, 0.0).astype(BF)
            stack.append(both * mask)
        spread[...] += nt_dot(jnp.concatenate(stack, axis=0), hot_t)
        return carry

    lax.fori_loop(0, leaves // UNROLL, scatter, 0)
    for b in range(leaves):
        at = b * 2 * rhs
        out[:, pl.ds(b * width, width)] = spread[pl.ds(at, rhs)] + spread[pl.ds(at + rhs, rhs)]


def local(points, charges, leaf_order, near_list, far_list, local_skel, upper_skel):
    features, total = points.shape
    rhs = charges.shape[0]
    leaves, _ = near_list.shape
    width = local_skel.shape[1]
    nodes = local_skel.shape[0]
    kern_scale = 2.0 * math.sqrt(3.0 / features)
    devices = lax.axis_size("leaf")
    upper = devices.bit_length() - 1
    depth = leaves.bit_length() - 1
    position = lax.axis_index("leaf")
    live = features + 2 * AUX
    rows = features + rhs
    shape = jax.ShapeDtypeStruct
    place = jnp.reshape(position, (1,)).astype(jnp.int32)

    half = leaves // 2
    fixed = sum(OWN_PARTS)
    most = near_list.size + max(half * half + half - 2, fixed)
    length = -(-(max(most, fixed + sum(ANY_PARTS)) + BATCH) // 128) * 128
    stacked, pairs = call(
        functools.partial(gather_kernel, fixed),
        (shape((rows, total), BF), shape((2, length), jnp.int32)),
        [HBM] * 5 + [SMEM],
        [
            pltpu.VMEM((leaves, rows, width), BF),
            pltpu.VMEM((leaves, width, width), BF),
            pltpu.VMEM((1, total), jnp.int32),
            pltpu.VMEM(near_list.shape, jnp.int32),
            pltpu.VMEM(far_list.shape, jnp.int32),
            pltpu.SemaphoreType.DMA((2 * leaves + 3,)),
        ],
        10**10,
        limit_mb=63,
    )(points, charges, leaf_order, near_list, far_list, place)
    within = lax.ppermute(stacked, "leaf", [(i, i ^ 1) for i in range(devices)])
    across = lax.ppermute(
        stacked, "leaf", [(i, i + 1 if i % 2 else i - 1) for i in range(1, devices - 1)]
    )
    known = leaves + nodes - 1
    srcs, tgts, wtss, kernels, own, own_tgt = call(
        functools.partial(tree_kernel, kern_scale, features),
        (
            shape((known, DEPTH, width), BF),
            shape((known, width, DEPTH), BF),
            shape((known, rhs, width), BF),
            shape((nodes, width, 2 * width), BF),
            shape((live + rhs, width), BF),
            shape((width, DEPTH), BF),
        ),
        [VMEM] * 2,
        [pltpu.VMEM((8, DEPTH, 2 * width), BF), pltpu.VMEM((8, rhs + 16, 2 * width), BF)],
        10**10,
    )(stacked, local_skel)

    def own_part(start, count, after, acc):
        return call(
            functools.partial(own_kernel, kern_scale, start, count),
            shape((known, rhs, width), F32),
            [SMEM] + [VMEM] * 3 + [ANY] + [VMEM] * (start > 0),
            [],
            10**10,
            aliases={5: 0} if start else None,
        )(pairs, srcs, tgts, wtss, after, *([acc] if start else []))

    def meet_part(start, count, after, acc):
        return call(
            functools.partial(meet_kernel, kern_scale, features, start, count),
            (
                shape((known, rhs, width), F32),
                shape((3 * leaves, DEPTH, width), BF),
                shape((3 * leaves, rhs, width), BF),
            ),
            [SMEM] * 2 + [VMEM] * 5 + [ANY, VMEM],
            [],
            10**10,
            aliases={8: 0},
        )(pairs, place, within, across, srcs, tgts, wtss, after, acc)

    def any_part(start, count, after, acc):
        return call(
            functools.partial(any_kernel, kern_scale, start, count),
            shape((known, rhs, width), F32),
            [SMEM] + [VMEM] * 3 + [ANY, VMEM],
            [],
            10**10,
            aliases={5: 0},
        )(pairs, all_src, tgts, all_wts, after, acc)

    siblings, targets, half_kernels = [], [], []
    acc = all_src = all_wts = None
    taken = 0
    for bit in range(upper):
        sibling = lax.ppermute(own, "leaf", [(i, i ^ (1 << bit)) for i in range(devices)])
        part = bit - len(OWN_PARTS)
        if part < 0:
            count = OWN_PARTS[bit]
            acc = own_part(taken, count, own, acc)
        elif part < len(ANY_PARTS):
            count = ANY_PARTS[part]
            if part == 0:
                acc, all_src, all_wts = meet_part(taken, count, own, acc)
            else:
                acc = any_part(taken, count, own, acc)
        else:
            count = 0
        taken += count
        siblings.append(sibling)
        targets.append(own_tgt)
        if bit == upper - 1:
            break
        own, own_tgt, half_kernel = call(
            functools.partial(chain_kernel, kern_scale, features, bit, devices),
            (
                shape((live + rhs, width), BF),
                shape((width, DEPTH), BF),
                shape((width, width), BF),
            ),
            [SMEM] + [VMEM] * 3 + [ANY],
            [pltpu.VMEM((DEPTH, 2 * width), BF), pltpu.VMEM((rhs + 16, 2 * width), BF)],
            10**8,
        )(place, own, sibling, upper_skel, acc)
        half_kernels.append(half_kernel)

    root, leaf_field = call(
        functools.partial(down_kernel, kern_scale, upper, live),
        (shape((rhs, width), F32), shape((leaves, rhs, width), F32)),
        [VMEM] * (2 + 3 * upper - 1),
        [],
        10**9,
    )(kernels, acc, *siblings, *targets, *half_kernels)

    potentials = call(
        functools.partial(final_kernel, kern_scale, taken),
        shape((rhs, total), F32),
        [SMEM] + [VMEM] * 6,
        [pltpu.VMEM((leaves, rhs, width), F32), pltpu.VMEM((leaves * 2 * rhs, width), F32)],
        10**10,
    )(pairs, all_src, tgts, all_wts, leaf_order, leaf_field, acc)
    return (potentials, root[None])


def solution(mesh):
    placed = (
        P(None, "leaf"),
        P(None, "leaf"),
        P("leaf", None),
        P("leaf", None),
        P("leaf", None),
        P("leaf", None),
        P(),
    )
    return jax.shard_map(
        local,
        mesh=mesh,
        in_specs=placed,
        out_specs=(P(None, "leaf"), P("leaf", None, None)),
        check_vma=False,
    )
```

```python
import functools
import math

import jax
import jax.numpy as jnp
from jax import lax
from jax.experimental import pallas as pl
from jax.experimental.pallas import tpu as pltpu
from jax.sharding import PartitionSpec as P

PAIR_GAIN = math.sqrt(2.0)
LOG2E = math.log2(math.e)
BF = jnp.bfloat16
F32 = jnp.float32
NT = (((1,), (1,)), ((), ()))
AUX = 8
PARTS = (0.25, 0.125)
ROW, BLOCK = 36, 12
OWN_ROWS = (2, 2)
ANY_ROWS = (1, 1, 1)
UNROLL = 4
VMEM = pl.BlockSpec(memory_space=pltpu.VMEM)
SMEM = pl.BlockSpec(memory_space=pltpu.SMEM)
HBM = pl.BlockSpec(memory_space=pltpu.HBM)
ANY = pl.BlockSpec(memory_space=pl.ANY)


def nt_dot(a, b):
    return lax.dot_general(a, b, NT, preferred_element_type=F32)


def nn_dot(a, b):
    return jnp.dot(a, b, preferred_element_type=F32)


def call(body, out_shape, in_specs, scratch, flops, out_specs=None, aliases=None, limit_mb=16):
    return pl.pallas_call(
        body,
        out_shape=out_shape,
        in_specs=in_specs,
        out_specs=out_specs or jax.tree.map(lambda _: VMEM, out_shape),
        input_output_aliases=aliases or {},
        scratch_shapes=scratch,
        compiler_params=pltpu.CompilerParams(vmem_limit_bytes=limit_mb * 2**20),
        cost_estimate=pl.CostEstimate(flops=flops, bytes_accessed=2**20, transcendentals=0),
    )


def kernel_tile(scaled):
    floor = jnp.maximum(scaled, 1e-30)
    t = floor * lax.rsqrt(floor)
    return ((t + 1.0) * jnp.exp2(t * -LOG2E)).astype(BF)


def aux_rows(x):
    features, width = x.shape
    norm = jnp.sum(x * x, axis=0, keepdims=True) * (12.0 / features)
    high = norm.astype(BF).astype(F32)
    rest = norm - high
    mid = rest.astype(BF).astype(F32)
    low = rest - mid
    row = lax.broadcasted_iota(jnp.int32, (AUX, width), 0)
    norms = jnp.where(row == 0, high, jnp.where(row == 1, mid, jnp.where(row == 2, low, 0.0)))
    ones = jnp.where(row < 3, 1.0, 0.0)
    return norms, ones


def source_form(x, norms, ones):
    return jnp.concatenate([x, x, norms, ones], axis=0).astype(BF)


def target_form(x, norms, ones):
    first, second = PARTS
    return jnp.concatenate([-first * x, -second * x, ones, norms], axis=0).T.astype(BF)


def split_form(selected, features):
    return (
        selected[:features],
        selected[features : features + AUX],
        selected[features + AUX : features + 2 * AUX],
    )


def one_hot(chosen, height):
    width = chosen.shape[1]
    row = lax.broadcasted_iota(jnp.int32, (height, width), 0)
    return jnp.where(row == chosen, 1.0, 0.0).astype(BF)


def flat(table, size):
    rows, cols = table.shape
    entry = lax.broadcasted_iota(jnp.int32, (cols, size), 1)
    pick = jnp.where(entry % cols == lax.broadcasted_iota(jnp.int32, (cols, size), 0), 1.0, 0.0)
    every = nn_dot(table.astype(BF), pick.astype(BF))
    entry = lax.broadcasted_iota(jnp.int32, (rows, size), 1)
    row = lax.broadcasted_iota(jnp.int32, (rows, size), 0)
    return jnp.sum(jnp.where(entry // cols == row, every, 0.0), axis=0, keepdims=True)


def pair_list(near, far, first_leaf, rows, fixed):
    leaves, slots = near.shape
    nodes, _ = far.shape
    upper = nodes - 2
    near_size, far_size = leaves * slots, nodes * nodes
    size = -(-(near_size + far_size + upper) // 128) * 128
    rest = size - near_size - far_size
    row = lax.broadcasted_iota(jnp.int32, (nodes, nodes), 0)
    col = lax.broadcasted_iota(jnp.int32, (nodes, nodes), 1)
    seen = jnp.where(col == row + 1 - 2 * (row & 1), 1.0, 0.0)
    for s in range(far.shape[1]):
        seen = seen + jnp.where(far[:, s : s + 1] == col, 1.0, 0.0)
    here = jnp.where(near >= 0, near - (first_leaf - leaves), -1).astype(F32)
    column = lax.broadcasted_iota(jnp.int32, (1, size), 1)
    is_far = (column >= near_size) & (column < near_size + far_size)
    is_up = (column >= near_size + far_size) & (column < near_size + far_size + upper)
    near_h = jnp.concatenate([flat(here, near_size), jnp.full((1, size - near_size), -1.0, F32)], axis=1)
    times = jnp.concatenate(
        [jnp.zeros((1, near_size), F32), flat(seen, far_size + rest)], axis=1
    )
    from_far = column - near_size
    from_up = from_far - far_size
    node_first = 2 * leaves
    up_at = nodes + from_up
    sibling = up_at + 1 - 2 * (from_up & 1)
    source = jnp.where(
        is_far, node_first + from_far % nodes, jnp.where(is_up, node_first + sibling, 0)
    ).astype(F32) + jnp.where(column < near_size, near_h, 0.0)
    target = jnp.where(
        is_far, leaves + from_far // nodes, jnp.where(is_up, leaves + up_at, column // slots)
    ).astype(F32)
    times = jnp.where(is_far, times, jnp.where(is_up | (near_h >= 0), 1.0, 0.0))
    level = jnp.where(times > 0, 1.0, 0.0)
    first = jnp.where(is_far | is_up, level, 0.0)
    own = jnp.where((near_h >= leaves) & (near_h < 2 * leaves), 1.0, 0.0)
    other = level - first - own
    row = lax.broadcasted_iota(jnp.int32, (16, size), 0)
    masks = jnp.where(row == 0, first, jnp.where(row == 1, own, jnp.where(row == 2, other, 0.0)))
    before = lax.broadcasted_iota(jnp.int32, (size, size), 1) < lax.broadcasted_iota(
        jnp.int32, (size, size), 0
    )
    rank = nt_dot(masks.astype(BF), jnp.where(before, 1.0, 0.0).astype(BF))
    found = jnp.sum(masks, axis=1, keepdims=True)
    start = jnp.maximum(found[0:1] + found[1:2], float(fixed))
    place = jnp.where(other > 0, start + rank[2:3], -1.0)
    place = jnp.where(own > 0, found[0:1] + rank[1:2], place)
    place = jnp.where(first > 0, rank[0:1], place)
    slot = lax.broadcasted_iota(jnp.int32, (rows * 128, size), 0)
    slot = jnp.where(slot % 128 < ROW, slot // 128 * ROW + slot % 128, -2).astype(F32)
    hit = jnp.where(slot == place, 1.0, 0.0).astype(BF)
    parts = jnp.where(row == 0, source, jnp.where(row == 1, target, jnp.where(row == 2, times, 0.0)))
    listed = nt_dot(parts.astype(BF), hit)
    code = (listed[0:1] + 256.0 * listed[1:2] + 65536.0 * listed[2:3]).astype(jnp.int32)
    code = jnp.where(listed[2:3] > 0.5, code, leaves)
    total = jnp.broadcast_to(start + found[2:3], (1, 128)).astype(jnp.int32)
    return jnp.concatenate([code[:, 128 * r : 128 * (r + 1)] for r in range(rows)] + [total], axis=0)


def gather_kernel(
    fixed, points, charges, order, near, far, place, stacked, pairs, grid, hots, index, slots, far_slots, sems
):
    features, total = points.shape
    rows = stacked.shape[0]
    width = hots.shape[1]
    blocks = grid.shape[0]
    fetch_index = pltpu.make_async_copy(order, index, sems.at[2 * blocks])
    fetch_index.start()
    fetches = []
    for b in range(blocks):
        cols = pl.ds(b * width, width)
        into = grid.at[b, pl.ds(0, features)]
        fetches.append(pltpu.make_async_copy(points.at[:, cols], into, sems.at[2 * b]))
        into = grid.at[b, pl.ds(features, rows - features)]
        fetches.append(pltpu.make_async_copy(charges.at[:, cols], into, sems.at[2 * b + 1]))
    fetch_slots = pltpu.make_async_copy(near, slots, sems.at[2 * blocks + 1])
    fetch_slots.start()
    fetch_far = pltpu.make_async_copy(far, far_slots, sems.at[2 * blocks + 2])
    fetch_far.start()
    for fetch in fetches:
        fetch.start()
    fetch_index.wait()
    for b in range(blocks):
        hots[b] = one_hot(index[:, pl.ds(b * width, width)] & (width - 1), width)
    fetch_slots.wait()
    fetch_far.wait()
    pairs[...] = pair_list(slots[...], far_slots[...], place[0] * blocks, pairs.shape[0] - 1, fixed)
    for fetch in fetches:
        fetch.wait()

    def block(i, carry):
        for u in range(UNROLL):
            j = i * UNROLL + u
            start = pl.multiple_of(j * width, width)
            home = index[:, pl.ds(start, width)] // width
            spread = nn_dot(grid[...].reshape(blocks * rows, width), hots[j])
            found = spread[:rows]
            for b in range(1, blocks):
                found = jnp.where(home == b, spread[b * rows : (b + 1) * rows], found)
            stacked[:, pl.ds(start, width)] = found.astype(BF)
        return carry

    lax.fori_loop(0, blocks // UNROLL, block, 0)


def lift(sources, weights, target):
    kernel = kernel_tile(nn_dot(target, sources))
    sums = nt_dot(weights, kernel)
    rhs = weights.shape[0] - 16
    lifted = PAIR_GAIN * (sums[:rhs] / sums[rhs : rhs + 1])
    return kernel, lifted


def with_ones(weights):
    return jnp.concatenate([weights, jnp.ones((16, weights.shape[1]), weights.dtype)], axis=0)


def tree_kernel(
    features, stacked, skel, srcs, tgts, wtss, kernels, payload, top_tgt, joined, joined_w, hots,
):
    width = skel.shape[1]
    nodes = skel.shape[0]
    leaves = nodes + 1
    for leaf in range(leaves):
        cols = pl.ds(leaf * width, width)
        x = stacked[:features, cols].astype(F32)
        norms, ones = aux_rows(x)
        srcs[leaf] = source_form(x, norms, ones)
        tgts[leaf] = target_form(x, norms, ones)
        wtss[leaf] = stacked[features:, cols]
    live = features + 2 * AUX
    for row in range(nodes):
        slot = row % 8
        for side in range(2):
            joined[slot, :, side * width : (side + 1) * width] = srcs[2 * row + side]
            joined_w[slot, :, side * width : (side + 1) * width] = with_ones(wtss[2 * row + side])
        hots[slot] = one_hot(skel[row : row + 1, :], 2 * width)
        x, norms, ones = split_form(nn_dot(joined[slot, features:], hots[slot]), features)
        own_src = source_form(x, norms, ones)
        own_tgt = target_form(x, norms, ones)
        kernel, lifted = lift(joined[slot], joined_w[slot], own_tgt)
        kernels[row] = kernel
        own_wts = lifted.astype(BF)
        if row < nodes - 1:
            srcs[leaves + row], tgts[leaves + row], wtss[leaves + row] = own_src, own_tgt, own_wts
        else:
            payload[:live] = own_src[features:]
            payload[live:] = own_wts
            top_tgt[...] = own_tgt


def both_parts(rows):
    return jnp.concatenate([rows[: rows.shape[0] - 2 * AUX], rows], axis=0)


def chain_kernel(
    features, bit, devices, place, own, sibling, skel, _, next_own, next_tgt, half_kernel, joined, joined_w, hot
):
    live = features + 2 * AUX
    width = own.shape[1]
    joined[:, :width] = both_parts(own[:live])
    joined[:, width:] = both_parts(sibling[:live])
    joined_w[:, :width] = with_ones(own[live:])
    joined_w[:, width:] = with_ones(sibling[live:])
    chosen = skel[pl.ds(devices - (devices >> bit) + (place[0] >> (bit + 1)), 1), :]
    chosen = chosen + ((place[0] >> bit) & 1) * jnp.where(chosen < width, width, -width)
    hot[...] = one_hot(chosen, 2 * width)
    x, norms, ones = split_form(nn_dot(joined[features:], hot[...]), features)
    target = target_form(x, norms, ones)
    kernel, lifted = lift(joined[...], joined_w[...], target)
    half_kernel[...] = kernel[:, :width]
    next_tgt[...] = target
    next_own[:live] = source_form(x, norms, ones)[features:]
    next_own[live:] = lifted.astype(BF)


def pair_terms(codes, src, tgt, wts, acc, first=0):
    terms = []
    for code in codes:
        h = (code & 255) - first
        g = (code >> 8) & 255
        times = (code >> 16).astype(F32)
        kernel = kernel_tile(nn_dot(tgt[g], src[h]))
        terms.append((g, nt_dot(wts[h], kernel) * times))
    for g, term in terms:
        acc[g] = acc[g] + term


def row_pairs(pairs, row, lanes, src, tgt, wts, acc, first=0):
    codes = pairs[pl.ds(row, 1), :]
    pair_terms([codes[0, u] for u in lanes], src, tgt, wts, acc, first)


def rows_of_pairs(start, count, pairs, src, tgt, wts, acc, first=0):
    def step(i, carry):
        row_pairs(pairs, start + i, range(ROW), src, tgt, wts, acc, first)
        return carry

    lax.fori_loop(0, count, step, 0)


def own_kernel(start, count, pairs, src, tgt, wts, _, *rest):
    acc = rest[-1]
    if start == 0:
        acc[...] = jnp.zeros_like(acc)
    rows_of_pairs(start, count, pairs, src, tgt, wts, acc, (src.shape[0] + 2) // 2)


def meet_kernel(
    features, start, count, pairs, place, within, across, own_src, tgt, own_wts, _, _acc,
    acc, src, wts,
):
    leaves = src.shape[0] // 3
    width = src.shape[2]
    odd = place[0] & 1
    for halo, side in ((within, 2 - 2 * odd), (across, 2 * odd)):
        for leaf in range(leaves):
            cols = pl.ds(leaf * width, width)
            x = halo[:features, cols].astype(F32)
            at = side * leaves + leaf
            src[at] = source_form(x, *aux_rows(x))
            wts[at] = halo[features:, cols]
    src[pl.ds(leaves, leaves)] = own_src[pl.ds(0, leaves)]
    wts[pl.ds(leaves, leaves)] = own_wts[pl.ds(0, leaves)]
    rows_of_pairs(start, count, pairs, src, tgt, wts, acc)


def any_kernel(start, count, pairs, src, tgt, wts, _, _acc, acc):
    rows_of_pairs(start, count, pairs, src, tgt, wts, acc)


def finish_kernel(upper, live, taken, pairs, src, tgt, wts, order, all_acc, kernels, *rest):
    siblings = rest[:upper]
    targets = rest[upper : 2 * upper]
    half_kernels = rest[2 * upper : 3 * upper - 1]
    out, root, leaf_field, acc, spread = rest[3 * upper - 1 :]
    width = root.shape[1]
    nodes = kernels.shape[0]
    leaves = nodes + 1
    rhs = root.shape[0]

    def push(field, kernel):
        sums = nn_dot(with_ones(field.astype(BF)), kernel)
        return sums[:rhs] / sums[rhs : rhs + 1]

    acc[...] = all_acc[pl.ds(0, leaves)]
    coupled = []
    for bit in range(upper):
        kernel = kernel_tile(nn_dot(targets[bit][...], both_parts(siblings[bit][:live])))
        coupled.append(nt_dot(siblings[bit][live:], kernel))
    field = coupled[upper - 1]
    for bit in range(upper - 2, -1, -1):
        field = coupled[bit] + push(field, half_kernels[bit][...])
    root[...] = field
    fields = {nodes - 1: field}
    for row in range(nodes - 1, -1, -1):
        pushed = push(fields[row], kernels[row])
        for side in range(2):
            below = 2 * row + side
            passed = pushed[:, side * width : (side + 1) * width]
            if below < leaves:
                leaf_field[below] = passed
            else:
                fields[below - leaves] = all_acc[below] + passed
    row_pairs(pairs, taken, range(2 * BLOCK), src, tgt, wts, acc)
    last = pairs.shape[0] - 1
    total = pairs[last : last + 1, :][0, 0]
    for row in range(taken, last):
        for first in range(2 * BLOCK if row == taken else 0, ROW, BLOCK):

            @pl.when(total > row * ROW + first)
            def _():
                row_pairs(pairs, row, range(first, first + BLOCK), src, tgt, wts, acc)

    spread[...] = jnp.zeros_like(spread)
    span = UNROLL * width

    def scatter(i, carry):
        index = order[:, pl.ds(pl.multiple_of(i * span, span), span)]
        home = index // width
        hot_t = one_hot(index & (width - 1), width)
        at = [i * UNROLL + u for u in range(UNROLL)]
        rows = jnp.concatenate([acc[leaf] + leaf_field[leaf] for leaf in at], axis=1)
        high = rows.astype(BF)
        low = (rows - high.astype(F32)).astype(BF)
        both = jnp.concatenate([high, low], axis=0)
        stack = []
        for b in range(leaves):
            mask = jnp.where(home == b, 1.0, 0.0).astype(BF)
            stack.append(both * mask)
        spread[...] += nt_dot(jnp.concatenate(stack, axis=0), hot_t)
        return carry

    lax.fori_loop(0, leaves // UNROLL, scatter, 0)
    for b in range(leaves):
        at = b * 2 * rhs
        out[:, pl.ds(b * width, width)] = spread[pl.ds(at, rhs)] + spread[pl.ds(at + rhs, rhs)]


def local(points, charges, leaf_order, near_list, far_list, local_skel, upper_skel):
    features, total = points.shape
    rhs = charges.shape[0]
    leaves, _ = near_list.shape
    width = local_skel.shape[1]
    nodes = local_skel.shape[0]
    devices = lax.axis_size("leaf")
    upper = devices.bit_length() - 1
    position = lax.axis_index("leaf")
    live = features + 2 * AUX
    depth = features + live
    rows = features + rhs
    assert 24 / features == sum(PARTS)
    shape = jax.ShapeDtypeStruct
    place = jnp.reshape(position, (1,)).astype(jnp.int32)

    half = leaves // 2
    fixed = sum(OWN_ROWS) * ROW
    most = near_list.size + max(half * half + half - 2, fixed)
    list_rows = max(-(-most // ROW), sum(OWN_ROWS + ANY_ROWS) + 1)
    stacked, pairs = call(
        functools.partial(gather_kernel, fixed),
        (shape((rows, total), BF), shape((list_rows + 1, 128), jnp.int32)),
        [HBM] * 5 + [SMEM],
        [
            pltpu.VMEM((leaves, rows, width), BF),
            pltpu.VMEM((leaves, width, width), BF),
            pltpu.VMEM((1, total), jnp.int32),
            pltpu.VMEM(near_list.shape, jnp.int32),
            pltpu.VMEM(far_list.shape, jnp.int32),
            pltpu.SemaphoreType.DMA((2 * leaves + 3,)),
        ],
        10**10,
        limit_mb=63,
    )(points, charges, leaf_order, near_list, far_list, place)
    within = lax.ppermute(stacked, "leaf", [(i, i ^ 1) for i in range(devices)])
    across = lax.ppermute(
        stacked, "leaf", [(i, i + 1 if i % 2 else i - 1) for i in range(1, devices - 1)]
    )
    known = leaves + nodes - 1
    srcs, tgts, wtss, kernels, own, own_tgt = call(
        functools.partial(tree_kernel, features),
        (
            shape((known, depth, width), BF),
            shape((known, width, depth), BF),
            shape((known, rhs, width), BF),
            shape((nodes, width, 2 * width), BF),
            shape((live + rhs, width), BF),
            shape((width, depth), BF),
        ),
        [VMEM] * 2,
        [
            pltpu.VMEM((8, depth, 2 * width), BF),
            pltpu.VMEM((8, rhs + 16, 2 * width), BF),
            pltpu.VMEM((8, 2 * width, width), BF),
        ],
        10**10,
    )(stacked, local_skel)

    def own_part(start, count, after, acc):
        return call(
            functools.partial(own_kernel, start, count),
            shape((known, rhs, width), F32),
            [VMEM] * 4 + [ANY] + [VMEM] * (start > 0),
            [],
            10**10,
            aliases={5: 0} if start else None,
        )(pairs, srcs, tgts, wtss, after, *([acc] if start else []))

    def meet_part(start, count, after, acc):
        return call(
            functools.partial(meet_kernel, features, start, count),
            (
                shape((known, rhs, width), F32),
                shape((3 * leaves, depth, width), BF),
                shape((3 * leaves, rhs, width), BF),
            ),
            [VMEM, SMEM] + [VMEM] * 5 + [ANY, VMEM],
            [],
            10**10,
            aliases={8: 0},
        )(pairs, place, within, across, srcs, tgts, wtss, after, acc)

    def any_part(start, count, after, acc):
        return call(
            functools.partial(any_kernel, start, count),
            shape((known, rhs, width), F32),
            [VMEM] * 4 + [ANY, VMEM],
            [],
            10**10,
            aliases={5: 0},
        )(pairs, all_src, tgts, all_wts, after, acc)

    siblings, targets, half_kernels = [], [], []
    acc = all_src = all_wts = None
    taken = 0
    for bit in range(upper):
        sibling = lax.ppermute(own, "leaf", [(i, i ^ (1 << bit)) for i in range(devices)])
        part = bit - len(OWN_ROWS)
        if part < 0:
            count = OWN_ROWS[bit]
            acc = own_part(taken, count, own, acc)
        elif part < len(ANY_ROWS):
            count = ANY_ROWS[part]
            if part == 0:
                acc, all_src, all_wts = meet_part(taken, count, own, acc)
            else:
                acc = any_part(taken, count, own, acc)
        else:
            count = 0
        taken += count
        siblings.append(sibling)
        targets.append(own_tgt)
        if bit == upper - 1:
            break
        own, own_tgt, half_kernel = call(
            functools.partial(chain_kernel, features, bit, devices),
            (
                shape((live + rhs, width), BF),
                shape((width, depth), BF),
                shape((width, width), BF),
            ),
            [SMEM] + [VMEM] * 3 + [ANY],
            [
                pltpu.VMEM((depth, 2 * width), BF),
                pltpu.VMEM((rhs + 16, 2 * width), BF),
                pltpu.VMEM((2 * width, width), BF),
            ],
            10**8,
        )(place, own, sibling, upper_skel, acc)
        half_kernels.append(half_kernel)

    potentials, root = call(
        functools.partial(finish_kernel, upper, live, taken),
        (shape((rhs, total), F32), shape((rhs, width), F32)),
        [VMEM] * (7 + 3 * upper - 1),
        [
            pltpu.VMEM((leaves, rhs, width), F32),
            pltpu.VMEM((leaves, rhs, width), F32),
            pltpu.VMEM((leaves * 2 * rhs, width), F32),
        ],
        10**10,
    )(pairs, all_src, tgts, all_wts, leaf_order, acc, kernels, *siblings, *targets, *half_kernels)
    return (potentials, root[None])


def solution(mesh):
    placed = (
        P(None, "leaf"),
        P(None, "leaf"),
        P("leaf", None),
        P("leaf", None),
        P("leaf", None),
        P("leaf", None),
        P(),
    )
    return jax.shard_map(
        local,
        mesh=mesh,
        in_specs=placed,
        out_specs=(P(None, "leaf"), P("leaf", None, None)),
        check_vma=False,
    )
```

```python
import functools
import math

import jax
import jax.numpy as jnp
from jax import lax
from jax.experimental import pallas as pl
from jax.experimental.pallas import tpu as pltpu
from jax.sharding import PartitionSpec as P

PAIR_GAIN = math.sqrt(2.0)
LOG2E = math.log2(math.e)
BF = jnp.bfloat16
F32 = jnp.float32
NT = (((1,), (1,)), ((), ()))
AUX = 8
PARTS = (0.25, 0.125)
ROW, BLOCK = 36, 12
OWN_ROWS = (2, 2)
ANY_ROWS = (1, 1, 1)
UNROLL = 4
VMEM = pl.BlockSpec(memory_space=pltpu.VMEM)
SMEM = pl.BlockSpec(memory_space=pltpu.SMEM)
HBM = pl.BlockSpec(memory_space=pltpu.HBM)
ANY = pl.BlockSpec(memory_space=pl.ANY)


def nt_dot(a, b):
    return lax.dot_general(a, b, NT, preferred_element_type=F32)


def nn_dot(a, b):
    return jnp.dot(a, b, preferred_element_type=F32)


def call(body, out_shape, in_specs, scratch, flops, out_specs=None, aliases=None, limit_mb=16):
    return pl.pallas_call(
        body,
        out_shape=out_shape,
        in_specs=in_specs,
        out_specs=out_specs or jax.tree.map(lambda _: VMEM, out_shape),
        input_output_aliases=aliases or {},
        scratch_shapes=scratch,
        compiler_params=pltpu.CompilerParams(vmem_limit_bytes=limit_mb * 2**20),
        cost_estimate=pl.CostEstimate(flops=flops, bytes_accessed=2**20, transcendentals=0),
    )


def kernel_tile(scaled):
    floor = jnp.maximum(scaled, 1e-30)
    t = floor * lax.rsqrt(floor)
    return ((t + 1.0) * jnp.exp2(t * -LOG2E)).astype(BF)


def aux_rows(x):
    features, width = x.shape
    norm = jnp.sum(x * x, axis=0, keepdims=True) * (12.0 / features)
    high = norm.astype(BF).astype(F32)
    rest = norm - high
    mid = rest.astype(BF).astype(F32)
    low = rest - mid
    row = lax.broadcasted_iota(jnp.int32, (AUX, width), 0)
    norms = jnp.where(row == 0, high, jnp.where(row == 1, mid, jnp.where(row == 2, low, 0.0)))
    ones = jnp.where(row < 3, 1.0, 0.0)
    return norms, ones


def source_form(x, norms, ones):
    return jnp.concatenate([x, x, norms, ones], axis=0).astype(BF)


def target_form(x, norms, ones):
    first, second = PARTS
    return jnp.concatenate([-first * x, -second * x, ones, norms], axis=0).T.astype(BF)


def split_form(selected, features):
    return (
        selected[:features],
        selected[features : features + AUX],
        selected[features + AUX : features + 2 * AUX],
    )


def one_hot(chosen, height):
    width = chosen.shape[1]
    row = lax.broadcasted_iota(jnp.int32, (height, width), 0)
    return jnp.where(row == chosen, 1.0, 0.0).astype(BF)


def flat(table, size):
    rows, cols = table.shape
    entry = lax.broadcasted_iota(jnp.int32, (cols, size), 1)
    pick = jnp.where(entry % cols == lax.broadcasted_iota(jnp.int32, (cols, size), 0), 1.0, 0.0)
    every = nn_dot(table.astype(BF), pick.astype(BF))
    entry = lax.broadcasted_iota(jnp.int32, (rows, size), 1)
    row = lax.broadcasted_iota(jnp.int32, (rows, size), 0)
    return jnp.sum(jnp.where(entry // cols == row, every, 0.0), axis=0, keepdims=True)


def pair_list(near, far, first_leaf, rows, fixed):
    leaves, slots = near.shape
    nodes, _ = far.shape
    upper = nodes - 2
    near_size, far_size = leaves * slots, nodes * nodes
    size = -(-(near_size + far_size + upper) // 128) * 128
    rest = size - near_size - far_size
    row = lax.broadcasted_iota(jnp.int32, (nodes, nodes), 0)
    col = lax.broadcasted_iota(jnp.int32, (nodes, nodes), 1)
    seen = jnp.where(col == row + 1 - 2 * (row & 1), 1.0, 0.0)
    for s in range(far.shape[1]):
        seen = seen + jnp.where(far[:, s : s + 1] == col, 1.0, 0.0)
    here = jnp.where(near >= 0, near - (first_leaf - leaves), -1).astype(F32)
    column = lax.broadcasted_iota(jnp.int32, (1, size), 1)
    is_far = (column >= near_size) & (column < near_size + far_size)
    is_up = (column >= near_size + far_size) & (column < near_size + far_size + upper)
    near_h = jnp.concatenate([flat(here, near_size), jnp.full((1, size - near_size), -1.0, F32)], axis=1)
    times = jnp.concatenate(
        [jnp.zeros((1, near_size), F32), flat(seen, far_size + rest)], axis=1
    )
    from_far = column - near_size
    from_up = from_far - far_size
    node_first = 2 * leaves
    up_at = nodes + from_up
    sibling = up_at + 1 - 2 * (from_up & 1)
    source = jnp.where(
        is_far, node_first + from_far % nodes, jnp.where(is_up, node_first + sibling, 0)
    ).astype(F32) + jnp.where(column < near_size, near_h, 0.0)
    target = jnp.where(
        is_far, leaves + from_far // nodes, jnp.where(is_up, leaves + up_at, column // slots)
    ).astype(F32)
    times = jnp.where(is_far, times, jnp.where(is_up | (near_h >= 0), 1.0, 0.0))
    level = jnp.where(times > 0, 1.0, 0.0)
    first = jnp.where(is_far | is_up, level, 0.0)
    own = jnp.where((near_h >= leaves) & (near_h < 2 * leaves), 1.0, 0.0)
    other = level - first - own
    row = lax.broadcasted_iota(jnp.int32, (16, size), 0)
    masks = jnp.where(row == 0, first, jnp.where(row == 1, own, jnp.where(row == 2, other, 0.0)))
    before = lax.broadcasted_iota(jnp.int32, (size, size), 1) < lax.broadcasted_iota(
        jnp.int32, (size, size), 0
    )
    rank = nt_dot(masks.astype(BF), jnp.where(before, 1.0, 0.0).astype(BF))
    found = jnp.sum(masks, axis=1, keepdims=True)
    start = jnp.maximum(found[0:1] + found[1:2], float(fixed))
    place = jnp.where(other > 0, start + rank[2:3], -1.0)
    place = jnp.where(own > 0, found[0:1] + rank[1:2], place)
    place = jnp.where(first > 0, rank[0:1], place)
    slot = lax.broadcasted_iota(jnp.int32, (rows * 128, size), 0)
    slot = jnp.where(slot % 128 < ROW, slot // 128 * ROW + slot % 128, -2).astype(F32)
    hit = jnp.where(slot == place, 1.0, 0.0).astype(BF)
    parts = jnp.where(row == 0, source, jnp.where(row == 1, target, jnp.where(row == 2, times, 0.0)))
    listed = nt_dot(parts.astype(BF), hit)
    code = (listed[0:1] + 256.0 * listed[1:2] + 65536.0 * listed[2:3]).astype(jnp.int32)
    code = jnp.where(listed[2:3] > 0.5, code, leaves)
    total = jnp.broadcast_to(start + found[2:3], (1, 128)).astype(jnp.int32)
    return jnp.concatenate([code[:, 128 * r : 128 * (r + 1)] for r in range(rows)] + [total], axis=0)


def gather_kernel(
    fixed, points, charges, order, near, far, place, stacked, pairs, grid, hots, index, slots, far_slots, sems
):
    features, total = points.shape
    rows = stacked.shape[0]
    width = hots.shape[1]
    blocks = grid.shape[0]
    fetch_index = pltpu.make_async_copy(order, index, sems.at[2 * blocks])
    fetch_index.start()
    fetches = []
    for b in range(blocks):
        cols = pl.ds(b * width, width)
        into = grid.at[b, pl.ds(0, features)]
        fetches.append(pltpu.make_async_copy(points.at[:, cols], into, sems.at[2 * b]))
        into = grid.at[b, pl.ds(features, rows - features)]
        fetches.append(pltpu.make_async_copy(charges.at[:, cols], into, sems.at[2 * b + 1]))
    fetch_slots = pltpu.make_async_copy(near, slots, sems.at[2 * blocks + 1])
    fetch_slots.start()
    fetch_far = pltpu.make_async_copy(far, far_slots, sems.at[2 * blocks + 2])
    fetch_far.start()
    for fetch in fetches:
        fetch.start()
    fetch_index.wait()
    for b in range(blocks):
        hots[b] = one_hot(index[:, pl.ds(b * width, width)] & (width - 1), width)
    fetch_slots.wait()
    fetch_far.wait()
    pairs[...] = pair_list(slots[...], far_slots[...], place[0] * blocks, pairs.shape[0] - 1, fixed)
    for fetch in fetches:
        fetch.wait()

    def block(i, carry):
        for u in range(UNROLL):
            j = i * UNROLL + u
            start = pl.multiple_of(j * width, width)
            home = index[:, pl.ds(start, width)] // width
            spread = nn_dot(grid[...].reshape(blocks * rows, width), hots[j])
            found = spread[:rows]
            for b in range(1, blocks):
                found = jnp.where(home == b, spread[b * rows : (b + 1) * rows], found)
            stacked[:, pl.ds(start, width)] = found.astype(BF)
        return carry

    lax.fori_loop(0, blocks // UNROLL, block, 0)


def lift(sources, weights, target):
    kernel = kernel_tile(nn_dot(target, sources))
    sums = nt_dot(weights, kernel)
    rhs = weights.shape[0] - 16
    lifted = PAIR_GAIN * (sums[:rhs] / sums[rhs : rhs + 1])
    return kernel, lifted


def with_ones(weights):
    return jnp.concatenate([weights, jnp.ones((16, weights.shape[1]), weights.dtype)], axis=0)


def tree_kernel(
    features, stacked, skel, srcs, tgts, wtss, kernels, payload, top_tgt, joined, joined_w, hots,
):
    width = skel.shape[1]
    nodes = skel.shape[0]
    leaves = nodes + 1
    for leaf in range(leaves):
        cols = pl.ds(leaf * width, width)
        x = stacked[:features, cols].astype(F32)
        norms, ones = aux_rows(x)
        srcs[leaf] = source_form(x, norms, ones)
        tgts[leaf] = target_form(x, norms, ones)
        wtss[leaf] = stacked[features:, cols]
    live = features + 2 * AUX
    for row in range(nodes):
        slot = row % 8
        for side in range(2):
            joined[slot, :, side * width : (side + 1) * width] = srcs[2 * row + side]
            joined_w[slot, :, side * width : (side + 1) * width] = with_ones(wtss[2 * row + side])
        hots[slot] = one_hot(skel[row : row + 1, :], 2 * width)
        x, norms, ones = split_form(nn_dot(joined[slot, features:], hots[slot]), features)
        own_src = source_form(x, norms, ones)
        own_tgt = target_form(x, norms, ones)
        kernel, lifted = lift(joined[slot], joined_w[slot], own_tgt)
        kernels[row] = kernel
        own_wts = lifted.astype(BF)
        if row < nodes - 1:
            srcs[leaves + row], tgts[leaves + row], wtss[leaves + row] = own_src, own_tgt, own_wts
        else:
            payload[:live] = own_src[features:]
            payload[live:] = own_wts
            top_tgt[...] = own_tgt


def both_parts(rows):
    return jnp.concatenate([rows[: rows.shape[0] - 2 * AUX], rows], axis=0)


def chain_kernel(
    features, bit, devices, place, own, sibling, skel, _, next_own, next_tgt, half_kernel, joined, joined_w, hot
):
    live = features + 2 * AUX
    width = own.shape[1]
    joined[:, :width] = both_parts(own[:live])
    joined[:, width:] = both_parts(sibling[:live])
    joined_w[:, :width] = with_ones(own[live:])
    joined_w[:, width:] = with_ones(sibling[live:])
    chosen = skel[pl.ds(devices - (devices >> bit) + (place[0] >> (bit + 1)), 1), :]
    chosen = chosen + ((place[0] >> bit) & 1) * jnp.where(chosen < width, width, -width)
    hot[...] = one_hot(chosen, 2 * width)
    x, norms, ones = split_form(nn_dot(joined[features:], hot[...]), features)
    target = target_form(x, norms, ones)
    kernel, lifted = lift(joined[...], joined_w[...], target)
    half_kernel[...] = kernel[:, :width]
    next_tgt[...] = target
    next_own[:live] = source_form(x, norms, ones)[features:]
    next_own[live:] = lifted.astype(BF)


def pair_terms(codes, src, tgt, wts, acc, first=0):
    terms = []
    for code in codes:
        h = (code & 255) - first
        g = (code >> 8) & 255
        times = (code >> 16).astype(F32)
        kernel = kernel_tile(nn_dot(tgt[g], src[h]))
        terms.append((g, nt_dot(wts[h], kernel) * times))
    for g, term in terms:
        acc[g] = acc[g] + term


def row_pairs(pairs, row, lanes, src, tgt, wts, acc, first=0):
    codes = pairs[pl.ds(row, 1), :]
    pair_terms([codes[0, u] for u in lanes], src, tgt, wts, acc, first)


def rows_of_pairs(start, count, pairs, src, tgt, wts, acc, first=0):
    def step(i, carry):
        row_pairs(pairs, start + i, range(ROW), src, tgt, wts, acc, first)
        return carry

    lax.fori_loop(0, count, step, 0)


def own_kernel(start, count, pairs, src, tgt, wts, _, *rest):
    acc = rest[-1]
    if start == 0:
        acc[...] = jnp.zeros_like(acc)
    rows_of_pairs(start, count, pairs, src, tgt, wts, acc, (src.shape[0] + 2) // 2)


def meet_kernel(
    features, start, count, pairs, place, within, across, own_src, tgt, own_wts, _, _acc,
    acc, src, wts,
):
    leaves = src.shape[0] // 3
    width = src.shape[2]
    odd = place[0] & 1
    for halo, side in ((within, 2 - 2 * odd), (across, 2 * odd)):
        for leaf in range(leaves):
            cols = pl.ds(leaf * width, width)
            x = halo[:features, cols].astype(F32)
            at = side * leaves + leaf
            src[at] = source_form(x, *aux_rows(x))
            wts[at] = halo[features:, cols]
    src[pl.ds(leaves, leaves)] = own_src[pl.ds(0, leaves)]
    wts[pl.ds(leaves, leaves)] = own_wts[pl.ds(0, leaves)]
    rows_of_pairs(start, count, pairs, src, tgt, wts, acc)


def any_kernel(start, count, pairs, src, tgt, wts, _, _acc, acc):
    rows_of_pairs(start, count, pairs, src, tgt, wts, acc)


def finish_kernel(upper, live, taken, pairs, src, tgt, wts, order, all_acc, kernels, *rest):
    siblings = rest[:upper]
    targets = rest[upper : 2 * upper]
    half_kernels = rest[2 * upper : 3 * upper - 1]
    out, root, leaf_field, acc, spread = rest[3 * upper - 1 :]
    width = root.shape[1]
    nodes = kernels.shape[0]
    leaves = nodes + 1
    rhs = root.shape[0]

    def push(field, kernel):
        sums = nn_dot(with_ones(field.astype(BF)), kernel)
        return sums[:rhs] / sums[rhs : rhs + 1]

    acc[...] = all_acc[pl.ds(0, leaves)]
    coupled = []
    for bit in range(upper):
        kernel = kernel_tile(nn_dot(targets[bit][...], both_parts(siblings[bit][:live])))
        coupled.append(nt_dot(siblings[bit][live:], kernel))
    field = coupled[upper - 1]
    for bit in range(upper - 2, -1, -1):
        field = coupled[bit] + push(field, half_kernels[bit][...])
    root[...] = field
    fields = {nodes - 1: field}
    for row in range(nodes - 1, -1, -1):
        pushed = push(fields[row], kernels[row])
        for side in range(2):
            below = 2 * row + side
            passed = pushed[:, side * width : (side + 1) * width]
            if below < leaves:
                leaf_field[below] = passed
            else:
                fields[below - leaves] = all_acc[below] + passed
    row_pairs(pairs, taken, range(2 * BLOCK), src, tgt, wts, acc)
    last = pairs.shape[0] - 1
    total = pairs[last : last + 1, :][0, 0]

    def more(row, carry):
        for first in range(0, ROW, BLOCK):
            fresh = total > row * ROW + first
            if first < 2 * BLOCK:
                fresh = fresh & (row > taken)

            @pl.when(fresh)
            def _():
                row_pairs(pairs, row, range(first, first + BLOCK), src, tgt, wts, acc)

        return carry

    lax.fori_loop(taken, (total + (ROW - 1)) // ROW, more, 0)
    spread[...] = jnp.zeros_like(spread)
    span = UNROLL * width

    def scatter(i, carry):
        index = order[:, pl.ds(pl.multiple_of(i * span, span), span)]
        home = index // width
        hot_t = one_hot(index & (width - 1), width)
        at = [i * UNROLL + u for u in range(UNROLL)]
        rows = jnp.concatenate([acc[leaf] + leaf_field[leaf] for leaf in at], axis=1)
        high = rows.astype(BF)
        low = (rows - high.astype(F32)).astype(BF)
        both = jnp.concatenate([high, low], axis=0)
        stack = []
        for b in range(leaves):
            mask = jnp.where(home == b, 1.0, 0.0).astype(BF)
            stack.append(both * mask)
        spread[...] += nt_dot(jnp.concatenate(stack, axis=0), hot_t)
        return carry

    lax.fori_loop(0, leaves // UNROLL, scatter, 0)
    for b in range(leaves):
        at = b * 2 * rhs
        out[:, pl.ds(b * width, width)] = spread[pl.ds(at, rhs)] + spread[pl.ds(at + rhs, rhs)]


def local(points, charges, leaf_order, near_list, far_list, local_skel, upper_skel):
    features, total = points.shape
    rhs = charges.shape[0]
    leaves, _ = near_list.shape
    width = local_skel.shape[1]
    nodes = local_skel.shape[0]
    devices = lax.axis_size("leaf")
    upper = devices.bit_length() - 1
    position = lax.axis_index("leaf")
    live = features + 2 * AUX
    depth = features + live
    rows = features + rhs
    assert 24 / features == sum(PARTS)
    shape = jax.ShapeDtypeStruct
    place = jnp.reshape(position, (1,)).astype(jnp.int32)

    half = leaves // 2
    fixed = sum(OWN_ROWS) * ROW
    most = near_list.size + max(half * half + half - 2, fixed)
    list_rows = max(-(-most // ROW), sum(OWN_ROWS + ANY_ROWS) + 1)
    stacked, pairs = call(
        functools.partial(gather_kernel, fixed),
        (shape((rows, total), BF), shape((list_rows + 1, 128), jnp.int32)),
        [HBM] * 5 + [SMEM],
        [
            pltpu.VMEM((leaves, rows, width), BF),
            pltpu.VMEM((leaves, width, width), BF),
            pltpu.VMEM((1, total), jnp.int32),
            pltpu.VMEM(near_list.shape, jnp.int32),
            pltpu.VMEM(far_list.shape, jnp.int32),
            pltpu.SemaphoreType.DMA((2 * leaves + 3,)),
        ],
        10**10,
        limit_mb=63,
    )(points, charges, leaf_order, near_list, far_list, place)
    within = lax.ppermute(stacked, "leaf", [(i, i ^ 1) for i in range(devices)])
    across = lax.ppermute(
        stacked, "leaf", [(i, i + 1 if i % 2 else i - 1) for i in range(1, devices - 1)]
    )
    known = leaves + nodes - 1
    srcs, tgts, wtss, kernels, own, own_tgt = call(
        functools.partial(tree_kernel, features),
        (
            shape((known, depth, width), BF),
            shape((known, width, depth), BF),
            shape((known, rhs, width), BF),
            shape((nodes, width, 2 * width), BF),
            shape((live + rhs, width), BF),
            shape((width, depth), BF),
        ),
        [VMEM] * 2,
        [
            pltpu.VMEM((8, depth, 2 * width), BF),
            pltpu.VMEM((8, rhs + 16, 2 * width), BF),
            pltpu.VMEM((8, 2 * width, width), BF),
        ],
        10**10,
    )(stacked, local_skel)

    def own_part(start, count, after, acc):
        return call(
            functools.partial(own_kernel, start, count),
            shape((known, rhs, width), F32),
            [VMEM] * 4 + [ANY] + [VMEM] * (start > 0),
            [],
            10**10,
            aliases={5: 0} if start else None,
        )(pairs, srcs, tgts, wtss, after, *([acc] if start else []))

    def meet_part(start, count, after, acc):
        return call(
            functools.partial(meet_kernel, features, start, count),
            (
                shape((known, rhs, width), F32),
                shape((3 * leaves, depth, width), BF),
                shape((3 * leaves, rhs, width), BF),
            ),
            [VMEM, SMEM] + [VMEM] * 5 + [ANY, VMEM],
            [],
            10**10,
            aliases={8: 0},
        )(pairs, place, within, across, srcs, tgts, wtss, after, acc)

    def any_part(start, count, after, acc):
        return call(
            functools.partial(any_kernel, start, count),
            shape((known, rhs, width), F32),
            [VMEM] * 4 + [ANY, VMEM],
            [],
            10**10,
            aliases={5: 0},
        )(pairs, all_src, tgts, all_wts, after, acc)

    siblings, targets, half_kernels = [], [], []
    acc = all_src = all_wts = None
    taken = 0
    for bit in range(upper):
        sibling = lax.ppermute(own, "leaf", [(i, i ^ (1 << bit)) for i in range(devices)])
        part = bit - len(OWN_ROWS)
        if part < 0:
            count = OWN_ROWS[bit]
            acc = own_part(taken, count, own, acc)
        elif part < len(ANY_ROWS):
            count = ANY_ROWS[part]
            if part == 0:
                acc, all_src, all_wts = meet_part(taken, count, own, acc)
            else:
                acc = any_part(taken, count, own, acc)
        else:
            count = 0
        taken += count
        siblings.append(sibling)
        targets.append(own_tgt)
        if bit == upper - 1:
            break
        own, own_tgt, half_kernel = call(
            functools.partial(chain_kernel, features, bit, devices),
            (
                shape((live + rhs, width), BF),
                shape((width, depth), BF),
                shape((width, width), BF),
            ),
            [SMEM] + [VMEM] * 3 + [ANY],
            [
                pltpu.VMEM((depth, 2 * width), BF),
                pltpu.VMEM((rhs + 16, 2 * width), BF),
                pltpu.VMEM((2 * width, width), BF),
            ],
            10**8,
        )(place, own, sibling, upper_skel, acc)
        half_kernels.append(half_kernel)

    potentials, root = call(
        functools.partial(finish_kernel, upper, live, taken),
        (shape((rhs, total), F32), shape((rhs, width), F32)),
        [VMEM] * (7 + 3 * upper - 1),
        [
            pltpu.VMEM((leaves, rhs, width), F32),
            pltpu.VMEM((leaves, rhs, width), F32),
            pltpu.VMEM((leaves * 2 * rhs, width), F32),
        ],
        10**10,
    )(pairs, all_src, tgts, all_wts, leaf_order, acc, kernels, *siblings, *targets, *half_kernels)
    return (potentials, root[None])


def solution(mesh):
    placed = (
        P(None, "leaf"),
        P(None, "leaf"),
        P("leaf", None),
        P("leaf", None),
        P("leaf", None),
        P("leaf", None),
        P(),
    )
    return jax.shard_map(
        local,
        mesh=mesh,
        in_specs=placed,
        out_specs=(P(None, "leaf"), P("leaf", None, None)),
        check_vma=False,
    )
```

```python
import functools
import math

import jax
import jax.numpy as jnp
from jax import lax
from jax.experimental import pallas as pl
from jax.experimental.pallas import tpu as pltpu
from jax.sharding import PartitionSpec as P

PAIR_GAIN = math.sqrt(2.0)
LOG2E = math.log2(math.e)
BF = jnp.bfloat16
F32 = jnp.float32
NT = (((1,), (1,)), ((), ()))
AUX = 8
PARTS = (0.25, 0.125)
ROW, BLOCK = 36, 12
OWN_ROWS = (2, 2)
ANY_ROWS = (1, 1, 1)
UNROLL = 8
VMEM = pl.BlockSpec(memory_space=pltpu.VMEM)
SMEM = pl.BlockSpec(memory_space=pltpu.SMEM)
HBM = pl.BlockSpec(memory_space=pltpu.HBM)
ANY = pl.BlockSpec(memory_space=pl.ANY)


def nt_dot(a, b):
    return lax.dot_general(a, b, NT, preferred_element_type=F32)


def nn_dot(a, b):
    return jnp.dot(a, b, preferred_element_type=F32)


def call(body, out_shape, in_specs, scratch, flops, out_specs=None, aliases=None, limit_mb=16):
    return pl.pallas_call(
        body,
        out_shape=out_shape,
        in_specs=in_specs,
        out_specs=out_specs or jax.tree.map(lambda _: VMEM, out_shape),
        input_output_aliases=aliases or {},
        scratch_shapes=scratch,
        compiler_params=pltpu.CompilerParams(vmem_limit_bytes=limit_mb * 2**20),
        cost_estimate=pl.CostEstimate(flops=flops, bytes_accessed=2**20, transcendentals=0),
    )


def kernel_tile(scaled):
    floor = jnp.maximum(scaled, 1e-30)
    t = floor * lax.rsqrt(floor)
    return ((t + 1.0) * jnp.exp2(t * -LOG2E)).astype(BF)


def aux_rows(x):
    features, width = x.shape
    norm = jnp.sum(x * x, axis=0, keepdims=True) * (12.0 / features)
    high = norm.astype(BF).astype(F32)
    rest = norm - high
    mid = rest.astype(BF).astype(F32)
    low = rest - mid
    row = lax.broadcasted_iota(jnp.int32, (AUX, width), 0)
    norms = jnp.where(row == 0, high, jnp.where(row == 1, mid, jnp.where(row == 2, low, 0.0)))
    ones = jnp.where(row < 3, 1.0, 0.0)
    return norms, ones


def source_form(x, norms, ones):
    return jnp.concatenate([x, x, norms, ones], axis=0).astype(BF)


def target_form(x, norms, ones):
    first, second = PARTS
    return jnp.concatenate([-first * x, -second * x, ones, norms], axis=0).T.astype(BF)


def split_form(selected, features):
    return (
        selected[:features],
        selected[features : features + AUX],
        selected[features + AUX : features + 2 * AUX],
    )


def one_hot(chosen, height):
    width = chosen.shape[1]
    row = lax.broadcasted_iota(jnp.int32, (height, width), 0)
    return jnp.where(row == chosen, 1.0, 0.0).astype(BF)


def flat(table, size):
    rows, cols = table.shape
    entry = lax.broadcasted_iota(jnp.int32, (cols, size), 1)
    pick = jnp.where(entry % cols == lax.broadcasted_iota(jnp.int32, (cols, size), 0), 1.0, 0.0)
    every = nn_dot(table.astype(BF), pick.astype(BF))
    entry = lax.broadcasted_iota(jnp.int32, (rows, size), 1)
    row = lax.broadcasted_iota(jnp.int32, (rows, size), 0)
    return jnp.sum(jnp.where(entry // cols == row, every, 0.0), axis=0, keepdims=True)


def pair_list(near, far, first_leaf, rows, fixed):
    leaves, slots = near.shape
    nodes, _ = far.shape
    upper = nodes - 2
    near_size, far_size = leaves * slots, nodes * nodes
    size = -(-(near_size + far_size + upper) // 128) * 128
    rest = size - near_size - far_size
    row = lax.broadcasted_iota(jnp.int32, (nodes, nodes), 0)
    col = lax.broadcasted_iota(jnp.int32, (nodes, nodes), 1)
    seen = jnp.where(col == row + 1 - 2 * (row & 1), 1.0, 0.0)
    for s in range(far.shape[1]):
        seen = seen + jnp.where(far[:, s : s + 1] == col, 1.0, 0.0)
    here = jnp.where(near >= 0, near - (first_leaf - leaves), -1).astype(F32)
    column = lax.broadcasted_iota(jnp.int32, (1, size), 1)
    is_far = (column >= near_size) & (column < near_size + far_size)
    is_up = (column >= near_size + far_size) & (column < near_size + far_size + upper)
    near_h = jnp.concatenate([flat(here, near_size), jnp.full((1, size - near_size), -1.0, F32)], axis=1)
    times = jnp.concatenate(
        [jnp.zeros((1, near_size), F32), flat(seen, far_size + rest)], axis=1
    )
    from_far = column - near_size
    from_up = from_far - far_size
    node_first = 2 * leaves
    up_at = nodes + from_up
    sibling = up_at + 1 - 2 * (from_up & 1)
    source = jnp.where(
        is_far, node_first + from_far % nodes, jnp.where(is_up, node_first + sibling, 0)
    ).astype(F32) + jnp.where(column < near_size, near_h, 0.0)
    target = jnp.where(
        is_far, leaves + from_far // nodes, jnp.where(is_up, leaves + up_at, column // slots)
    ).astype(F32)
    times = jnp.where(is_far, times, jnp.where(is_up | (near_h >= 0), 1.0, 0.0))
    level = jnp.where(times > 0, 1.0, 0.0)
    first = jnp.where(is_far | is_up, level, 0.0)
    own = jnp.where((near_h >= leaves) & (near_h < 2 * leaves), 1.0, 0.0)
    other = level - first - own
    row = lax.broadcasted_iota(jnp.int32, (16, size), 0)
    masks = jnp.where(row == 0, first, jnp.where(row == 1, own, jnp.where(row == 2, other, 0.0)))
    before = lax.broadcasted_iota(jnp.int32, (size, size), 1) < lax.broadcasted_iota(
        jnp.int32, (size, size), 0
    )
    rank = nt_dot(masks.astype(BF), jnp.where(before, 1.0, 0.0).astype(BF))
    found = jnp.sum(masks, axis=1, keepdims=True)
    start = jnp.maximum(found[0:1] + found[1:2], float(fixed))
    place = jnp.where(other > 0, start + rank[2:3], -1.0)
    place = jnp.where(own > 0, found[0:1] + rank[1:2], place)
    place = jnp.where(first > 0, rank[0:1], place)
    slot = lax.broadcasted_iota(jnp.int32, (rows * 128, size), 0)
    slot = jnp.where(slot % 128 < ROW, slot // 128 * ROW + slot % 128, -2).astype(F32)
    hit = jnp.where(slot == place, 1.0, 0.0).astype(BF)
    parts = jnp.where(row == 0, source, jnp.where(row == 1, target, jnp.where(row == 2, times, 0.0)))
    listed = nt_dot(parts.astype(BF), hit)
    code = (listed[0:1] + 256.0 * listed[1:2] + 65536.0 * listed[2:3]).astype(jnp.int32)
    code = jnp.where(listed[2:3] > 0.5, code, leaves)
    total = jnp.broadcast_to(start + found[2:3], (1, 128)).astype(jnp.int32)
    return jnp.concatenate([code[:, 128 * r : 128 * (r + 1)] for r in range(rows)] + [total], axis=0)


def gather_kernel(
    fixed, points, charges, order, near, far, place, stacked, pairs, grid, hots, index, slots, far_slots, sems
):
    features, total = points.shape
    rows = stacked.shape[0]
    width = hots.shape[1]
    blocks = grid.shape[0]
    fetch_index = pltpu.make_async_copy(order, index, sems.at[2 * blocks])
    fetch_index.start()
    fetches = []
    for b in range(blocks):
        cols = pl.ds(b * width, width)
        into = grid.at[b, pl.ds(0, features)]
        fetches.append(pltpu.make_async_copy(points.at[:, cols], into, sems.at[2 * b]))
        into = grid.at[b, pl.ds(features, rows - features)]
        fetches.append(pltpu.make_async_copy(charges.at[:, cols], into, sems.at[2 * b + 1]))
    fetch_slots = pltpu.make_async_copy(near, slots, sems.at[2 * blocks + 1])
    fetch_slots.start()
    fetch_far = pltpu.make_async_copy(far, far_slots, sems.at[2 * blocks + 2])
    fetch_far.start()
    for fetch in fetches:
        fetch.start()
    fetch_index.wait()
    for b in range(blocks):
        hots[b] = one_hot(index[:, pl.ds(b * width, width)] & (width - 1), width)
    fetch_slots.wait()
    fetch_far.wait()
    pairs[...] = pair_list(slots[...], far_slots[...], place[0] * blocks, pairs.shape[0] - 1, fixed)
    for fetch in fetches:
        fetch.wait()

    def block(i, carry):
        for u in range(UNROLL):
            j = i * UNROLL + u
            start = pl.multiple_of(j * width, width)
            home = index[:, pl.ds(start, width)] // width
            spread = nn_dot(grid[...].reshape(blocks * rows, width), hots[j])
            found = spread[:rows]
            for b in range(1, blocks):
                found = jnp.where(home == b, spread[b * rows : (b + 1) * rows], found)
            stacked[:, pl.ds(start, width)] = found.astype(BF)
        return carry

    lax.fori_loop(0, blocks // UNROLL, block, 0)


def lift(weights, kernel):
    sums = nt_dot(weights, kernel)
    rhs = weights.shape[0] - 16
    return PAIR_GAIN * (sums[:rhs] / sums[rhs : rhs + 1])


def with_ones(weights):
    return jnp.concatenate([weights, jnp.ones((16, weights.shape[1]), weights.dtype)], axis=0)


def tree_kernel(
    features, stacked, skel, srcs, tgts, wtss, kernels, payload, top_tgt, joined, joined_w, hots,
):
    width = skel.shape[1]
    nodes = skel.shape[0]
    leaves = nodes + 1
    for leaf in range(leaves):
        cols = pl.ds(leaf * width, width)
        x = stacked[:features, cols].astype(F32)
        norms, ones = aux_rows(x)
        srcs[leaf] = source_form(x, norms, ones)
        tgts[leaf] = target_form(x, norms, ones)
        wtss[leaf] = stacked[features:, cols]
    live = features + 2 * AUX
    for row in range(nodes):
        for side in range(2):
            joined[row, :, side * width : (side + 1) * width] = srcs[2 * row + side]
        hots[row] = one_hot(skel[row : row + 1, :], 2 * width)
        x, norms, ones = split_form(nn_dot(joined[row, features:], hots[row]), features)
        own_src = source_form(x, norms, ones)
        own_tgt = target_form(x, norms, ones)
        if row < nodes - 1:
            srcs[leaves + row], tgts[leaves + row] = own_src, own_tgt
        else:
            payload[:live] = own_src[features:]
            top_tgt[...] = own_tgt
    for row in range(nodes):
        target = tgts[leaves + row] if row < nodes - 1 else top_tgt[...]
        kernels[row] = kernel_tile(nn_dot(target, joined[row]))
    for row in range(nodes):
        for side in range(2):
            joined_w[row, :, side * width : (side + 1) * width] = with_ones(wtss[2 * row + side])
        own_wts = lift(joined_w[row], kernels[row]).astype(BF)
        if row < nodes - 1:
            wtss[leaves + row] = own_wts
        else:
            payload[live:] = own_wts


def both_parts(rows):
    return jnp.concatenate([rows[: rows.shape[0] - 2 * AUX], rows], axis=0)


def chain_kernel(
    features, bit, devices, place, own, sibling, skel, _, next_own, next_tgt, half_kernel, joined, joined_w, hot
):
    live = features + 2 * AUX
    width = own.shape[1]
    joined[:, :width] = both_parts(own[:live])
    joined[:, width:] = both_parts(sibling[:live])
    joined_w[:, :width] = with_ones(own[live:])
    joined_w[:, width:] = with_ones(sibling[live:])
    chosen = skel[pl.ds(devices - (devices >> bit) + (place[0] >> (bit + 1)), 1), :]
    chosen = chosen + ((place[0] >> bit) & 1) * jnp.where(chosen < width, width, -width)
    hot[...] = one_hot(chosen, 2 * width)
    x, norms, ones = split_form(nn_dot(joined[features:], hot[...]), features)
    target = target_form(x, norms, ones)
    kernel = kernel_tile(nn_dot(target, joined[...]))
    lifted = lift(joined_w[...], kernel)
    half_kernel[...] = kernel[:, :width]
    next_tgt[...] = target
    next_own[:live] = source_form(x, norms, ones)[features:]
    next_own[live:] = lifted.astype(BF)


def pair_terms(codes, src, tgt, wts, acc, first=0):
    terms = []
    for code in codes:
        h = (code & 255) - first
        g = (code >> 8) & 255
        times = (code >> 16).astype(F32)
        kernel = kernel_tile(nn_dot(tgt[g], src[h]))
        terms.append((g, nt_dot(wts[h], kernel) * times))
    for g, term in terms:
        acc[g] = acc[g] + term


def row_pairs(pairs, row, lanes, src, tgt, wts, acc, first=0):
    codes = pairs[pl.ds(row, 1), :]
    pair_terms([codes[0, u] for u in lanes], src, tgt, wts, acc, first)


def rows_of_pairs(start, count, pairs, src, tgt, wts, acc, first=0):
    def step(i, carry):
        row_pairs(pairs, start + i, range(ROW), src, tgt, wts, acc, first)
        return carry

    lax.fori_loop(0, count, step, 0)


def own_kernel(start, count, pairs, src, tgt, wts, _, *rest):
    acc = rest[-1]
    if start == 0:
        acc[...] = jnp.zeros_like(acc)
    rows_of_pairs(start, count, pairs, src, tgt, wts, acc, (src.shape[0] + 2) // 2)


def meet_kernel(
    features, start, count, pairs, place, within, across, own_src, tgt, own_wts, _, _acc,
    acc, src, wts,
):
    leaves = src.shape[0] // 3
    width = src.shape[2]
    odd = place[0] & 1
    for halo, side in ((within, 2 - 2 * odd), (across, 2 * odd)):
        for leaf in range(leaves):
            cols = pl.ds(leaf * width, width)
            x = halo[:features, cols].astype(F32)
            at = side * leaves + leaf
            src[at] = source_form(x, *aux_rows(x))
            wts[at] = halo[features:, cols]
    src[pl.ds(leaves, leaves)] = own_src[pl.ds(0, leaves)]
    wts[pl.ds(leaves, leaves)] = own_wts[pl.ds(0, leaves)]
    rows_of_pairs(start, count, pairs, src, tgt, wts, acc)


def any_kernel(start, count, pairs, src, tgt, wts, _, _acc, acc):
    rows_of_pairs(start, count, pairs, src, tgt, wts, acc)


def finish_kernel(upper, live, taken, pairs, src, tgt, wts, order, all_acc, kernels, *rest):
    siblings = rest[:upper]
    targets = rest[upper : 2 * upper]
    half_kernels = rest[2 * upper : 3 * upper - 1]
    out, root, leaf_field, acc, spread = rest[3 * upper - 1 :]
    width = root.shape[1]
    nodes = kernels.shape[0]
    leaves = nodes + 1
    rhs = root.shape[0]

    def push(field, kernel):
        sums = nn_dot(with_ones(field.astype(BF)), kernel)
        return sums[:rhs] / sums[rhs : rhs + 1]

    acc[...] = all_acc[pl.ds(0, leaves)]
    coupled = []
    for bit in range(upper):
        kernel = kernel_tile(nn_dot(targets[bit][...], both_parts(siblings[bit][:live])))
        coupled.append(nt_dot(siblings[bit][live:], kernel))
    field = coupled[upper - 1]
    for bit in range(upper - 2, -1, -1):
        field = coupled[bit] + push(field, half_kernels[bit][...])
    root[...] = field
    fields = {nodes - 1: field}
    for row in range(nodes - 1, -1, -1):
        pushed = push(fields[row], kernels[row])
        for side in range(2):
            below = 2 * row + side
            passed = pushed[:, side * width : (side + 1) * width]
            if below < leaves:
                leaf_field[below] = passed
            else:
                fields[below - leaves] = all_acc[below] + passed
    row_pairs(pairs, taken, range(2 * BLOCK), src, tgt, wts, acc)
    last = pairs.shape[0] - 1
    total = pairs[last : last + 1, :][0, 0]

    def more(row, carry):
        for first in range(0, ROW, BLOCK):
            fresh = total > row * ROW + first
            if first < 2 * BLOCK:
                fresh = fresh & (row > taken)

            @pl.when(fresh)
            def _():
                row_pairs(pairs, row, range(first, first + BLOCK), src, tgt, wts, acc)

        return carry

    lax.fori_loop(taken, (total + (ROW - 1)) // ROW, more, 0)
    spread[...] = jnp.zeros_like(spread)
    span = UNROLL * width

    def scatter(i, carry):
        index = order[:, pl.ds(pl.multiple_of(i * span, span), span)]
        home = index // width
        hot_t = one_hot(index & (width - 1), width)
        at = [i * UNROLL + u for u in range(UNROLL)]
        rows = jnp.concatenate([acc[leaf] + leaf_field[leaf] for leaf in at], axis=1)
        high = rows.astype(BF)
        low = (rows - high.astype(F32)).astype(BF)
        both = jnp.concatenate([high, low], axis=0)
        stack = []
        for b in range(leaves):
            mask = jnp.where(home == b, 1.0, 0.0).astype(BF)
            stack.append(both * mask)
        spread[...] += nt_dot(jnp.concatenate(stack, axis=0), hot_t)
        return carry

    lax.fori_loop(0, leaves // UNROLL, scatter, 0)
    for b in range(leaves):
        at = b * 2 * rhs
        out[:, pl.ds(b * width, width)] = spread[pl.ds(at, rhs)] + spread[pl.ds(at + rhs, rhs)]


def local(points, charges, leaf_order, near_list, far_list, local_skel, upper_skel):
    features, total = points.shape
    rhs = charges.shape[0]
    leaves, _ = near_list.shape
    width = local_skel.shape[1]
    nodes = local_skel.shape[0]
    devices = lax.axis_size("leaf")
    upper = devices.bit_length() - 1
    position = lax.axis_index("leaf")
    live = features + 2 * AUX
    depth = features + live
    rows = features + rhs
    assert 24 / features == sum(PARTS)
    shape = jax.ShapeDtypeStruct
    place = jnp.reshape(position, (1,)).astype(jnp.int32)

    half = leaves // 2
    fixed = sum(OWN_ROWS) * ROW
    most = near_list.size + max(half * half + half - 2, fixed)
    list_rows = max(-(-most // ROW), sum(OWN_ROWS + ANY_ROWS) + 1)
    stacked, pairs = call(
        functools.partial(gather_kernel, fixed),
        (shape((rows, total), BF), shape((list_rows + 1, 128), jnp.int32)),
        [HBM] * 5 + [SMEM],
        [
            pltpu.VMEM((leaves, rows, width), BF),
            pltpu.VMEM((leaves, width, width), BF),
            pltpu.VMEM((1, total), jnp.int32),
            pltpu.VMEM(near_list.shape, jnp.int32),
            pltpu.VMEM(far_list.shape, jnp.int32),
            pltpu.SemaphoreType.DMA((2 * leaves + 3,)),
        ],
        10**10,
        limit_mb=63,
    )(points, charges, leaf_order, near_list, far_list, place)
    within = lax.ppermute(stacked, "leaf", [(i, i ^ 1) for i in range(devices)])
    across = lax.ppermute(
        stacked, "leaf", [(i, i + 1 if i % 2 else i - 1) for i in range(1, devices - 1)]
    )
    known = leaves + nodes - 1
    srcs, tgts, wtss, kernels, own, own_tgt = call(
        functools.partial(tree_kernel, features),
        (
            shape((known, depth, width), BF),
            shape((known, width, depth), BF),
            shape((known, rhs, width), BF),
            shape((nodes, width, 2 * width), BF),
            shape((live + rhs, width), BF),
            shape((width, depth), BF),
        ),
        [VMEM] * 2,
        [
            pltpu.VMEM((nodes, depth, 2 * width), BF),
            pltpu.VMEM((nodes, rhs + 16, 2 * width), BF),
            pltpu.VMEM((nodes, 2 * width, width), BF),
        ],
        10**10,
    )(stacked, local_skel)

    def own_part(start, count, after, acc):
        return call(
            functools.partial(own_kernel, start, count),
            shape((known, rhs, width), F32),
            [VMEM] * 4 + [ANY] + [VMEM] * (start > 0),
            [],
            10**10,
            aliases={5: 0} if start else None,
        )(pairs, srcs, tgts, wtss, after, *([acc] if start else []))

    def meet_part(start, count, after, acc):
        return call(
            functools.partial(meet_kernel, features, start, count),
            (
                shape((known, rhs, width), F32),
                shape((3 * leaves, depth, width), BF),
                shape((3 * leaves, rhs, width), BF),
            ),
            [VMEM, SMEM] + [VMEM] * 5 + [ANY, VMEM],
            [],
            10**10,
            aliases={8: 0},
        )(pairs, place, within, across, srcs, tgts, wtss, after, acc)

    def any_part(start, count, after, acc):
        return call(
            functools.partial(any_kernel, start, count),
            shape((known, rhs, width), F32),
            [VMEM] * 4 + [ANY, VMEM],
            [],
            10**10,
            aliases={5: 0},
        )(pairs, all_src, tgts, all_wts, after, acc)

    siblings, targets, half_kernels = [], [], []
    acc = all_src = all_wts = None
    taken = 0
    for bit in range(upper):
        sibling = lax.ppermute(own, "leaf", [(i, i ^ (1 << bit)) for i in range(devices)])
        part = bit - len(OWN_ROWS)
        if part < 0:
            count = OWN_ROWS[bit]
            acc = own_part(taken, count, own, acc)
        elif part < len(ANY_ROWS):
            count = ANY_ROWS[part]
            if part == 0:
                acc, all_src, all_wts = meet_part(taken, count, own, acc)
            else:
                acc = any_part(taken, count, own, acc)
        else:
            count = 0
        taken += count
        siblings.append(sibling)
        targets.append(own_tgt)
        if bit == upper - 1:
            break
        own, own_tgt, half_kernel = call(
            functools.partial(chain_kernel, features, bit, devices),
            (
                shape((live + rhs, width), BF),
                shape((width, depth), BF),
                shape((width, width), BF),
            ),
            [SMEM] + [VMEM] * 3 + [ANY],
            [
                pltpu.VMEM((depth, 2 * width), BF),
                pltpu.VMEM((rhs + 16, 2 * width), BF),
                pltpu.VMEM((2 * width, width), BF),
            ],
            10**8,
        )(place, own, sibling, upper_skel, acc)
        half_kernels.append(half_kernel)

    potentials, root = call(
        functools.partial(finish_kernel, upper, live, taken),
        (shape((rhs, total), F32), shape((rhs, width), F32)),
        [VMEM] * (7 + 3 * upper - 1),
        [
            pltpu.VMEM((leaves, rhs, width), F32),
            pltpu.VMEM((leaves, rhs, width), F32),
            pltpu.VMEM((leaves * 2 * rhs, width), F32),
        ],
        10**10,
    )(pairs, all_src, tgts, all_wts, leaf_order, acc, kernels, *siblings, *targets, *half_kernels)
    return (potentials, root[None])


def solution(mesh):
    placed = (
        P(None, "leaf"),
        P(None, "leaf"),
        P("leaf", None),
        P("leaf", None),
        P("leaf", None),
        P("leaf", None),
        P(),
    )
    return jax.shard_map(
        local,
        mesh=mesh,
        in_specs=placed,
        out_specs=(P(None, "leaf"), P("leaf", None, None)),
        check_vma=False,
    )
```
